256 devices in a mesh: particle: 32 (over y, x, core), tensor: 8 (over z).
Axes of the slice: x: 4, y: 4, z: 8, core: 2. Of those that a mesh axis runs over, the one named last changes fastest.
Arguments:
- queries: bfloat16 [1024, 2, 8192], P('particle', None, 'tensor'), may hold values from -30 to 30
- new_keys: bfloat16 [1024, 2, 1024], P('particle', None, 'tensor'), may hold values from -6 to 6
- new_values: bfloat16 [1024, 2, 1024], P('particle', None, 'tensor'), may hold values from -6 to 6
- key_cache: bfloat16 [1024, 256, 1024], P('particle', None, 'tensor'), may hold values from -6 to 6
- value_cache: bfloat16 [1024, 256, 1024], P('particle', None, 'tensor'), may hold values from -6 to 6
- prompt_keys: bfloat16 [2048, 1024], P('particle', 'tensor'), may hold values from -6 to 6
- prompt_values: bfloat16 [2048, 1024], P('particle', 'tensor'), may hold values from -6 to 6
- lengths: int32 [1024], P('particle'), may hold values from 1 to 254, as said below
- prior: float32 [1024], P('particle'), may hold values from -4 to 290
- reward_dir: float32 [8192], P('tensor'), may hold values from -6 to 6
- rungs: int32 [1024], replicated, may hold values from 0 to 7, as said below
- ancestors: int32 [1024], replicated, may hold values from 0 to 1023, as said below
Outputs:
- attention: bfloat16 [1024, 2, 8192], P('particle', None, 'tensor')
- weights: float32 [1024], P('particle')
- rung_means: float32 [8], replicated
- next_keys: bfloat16 [1024, 256, 1024], P('particle', None, 'tensor')
- next_values: bfloat16 [1024, 256, 1024], P('particle', None, 'tensor')
- next_lengths: int32 [1024], P('particle')
The draws below stay inside these ranges and needn't reach their ends.
Inputs may be any that keep to these rules, and one draw needn't show every extreme that they name: In each aligned block of 32 particles, at most 3 name ancestors in any one aligned block and at most 2 distinct ancestors lie in any one aligned block; in every block both bounds are reached for some source block. `lengths`: every aligned block of 32 particles holds a particle with 254 filled slots. `rungs`: every rung holds at least one particle.
All inputs are finite; a program needn't handle non-finite values.
Results may differ from the reference program's by a relative error of at most 0.0085.
Values may be sent and summed in bfloat16 or wider, within the bound.
No kernel may reach another device: no remote copies, remote signals or barrier semaphores. Data moves between devices by JAX's collectives and lax.ppermute only.
A program may use at most 128 MiB of HBM per device.

```python
import jax
import jax.numpy as jnp
from jax import lax

HEADS = 64
KV_HEADS = 8
HEAD_DIM = 128
PART_DEV = 32
PROMPT = 2048
SUFFIX = 256
STEPS = 2
RUNGS = 8
CAPACITY = 3
DISTINCT = 2
PARTICLES = 1024


def rung_table(key):
    count_key = jax.random.fold_in(key, 101)
    order_key = jax.random.fold_in(key, 102)
    table = jax.random.randint(count_key, (PARTICLES,), 0, RUNGS)
    order = jax.random.permutation(order_key, PARTICLES)
    return table.at[order[:RUNGS]].set(jnp.arange(RUNGS, dtype=jnp.int32)).astype(jnp.int32)


def draw_rungs(key, part):
    return rung_table(key)


def draw_prior(key, part):
    key = jax.random.fold_in(key, 7)
    index = jnp.arange(PARTICLES, dtype=jnp.float32)
    trend = jnp.log(1.0 + 2.0 * index / max(PARTICLES - 1, 1))
    noise = jnp.clip(jax.random.normal(key, (PARTICLES,), jnp.float32), -6.0, 6.0)
    return 0.5 * noise + trend


def draw_prompt_keys(key, part):
    key = jax.random.fold_in(key, 11)
    base = jax.random.normal(key, (PROMPT, KV_HEADS * HEAD_DIM), jnp.float32)
    return jnp.clip(base, -6.0, 6.0).astype(jnp.bfloat16)


def draw_queries(key, part):
    key = jax.random.fold_in(key, 13)
    base = jax.random.normal(key, (PARTICLES, STEPS, HEADS * HEAD_DIM), jnp.float32)
    return jnp.clip(base, -6.0, 6.0).astype(jnp.bfloat16)


def draw_lengths(key, part):
    key = jax.random.fold_in(key, 17)
    first_key, second_key = jax.random.split(key)
    blocks = PARTICLES // PART_DEV
    values = jax.random.randint(first_key, (blocks, PART_DEV), 1, SUFFIX - 1)
    column = jax.random.randint(second_key, (blocks,), 0, PART_DEV)
    values = jnp.where(jnp.arange(PART_DEV)[None, :] == column[:, None], SUFFIX - 2, values)
    return values.reshape(PARTICLES).astype(jnp.int32)


def draw_ancestors(key, part):
    key = jax.random.fold_in(key, 19)
    blocks = PARTICLES // PART_DEV
    most_full = PART_DEV // CAPACITY
    fewest = most_full
    for count in range(most_full, 0, -1):
        if count + (PART_DEV - count * CAPACITY + DISTINCT - 1) // DISTINCT <= blocks:
            fewest = count

    def one_block(block_key):
        keys = jax.random.split(block_key, 4)
        full = jax.random.randint(keys[0], (), fewest, most_full + 1)
        sources = jax.random.permutation(keys[1], blocks)
        orders = jax.vmap(lambda inner: jax.random.permutation(inner, PART_DEV))(jax.random.split(keys[2], blocks))
        row = jnp.arange(PART_DEV)
        head_rows = full * CAPACITY
        in_full = row < head_rows
        rest = jnp.maximum(row - head_rows, 0)
        source_slot = jnp.where(in_full, row // CAPACITY, full + rest // DISTINCT)
        within = jnp.where(in_full, jnp.maximum(row % CAPACITY - 1, 0), rest % DISTINCT)
        local = orders[source_slot, within]
        shuffle = jax.random.permutation(keys[3], PART_DEV)
        return (sources[source_slot] * PART_DEV + local)[shuffle]
    result = jax.vmap(one_block)(jax.random.split(key, blocks))
    return result.reshape(PARTICLES).astype(jnp.int32)


def steps_of(rng, dims, cuts, smallest, largest):
    gain = 1.0
    for dim, blocks in cuts:
        steps = jax.random.uniform(jax.random.fold_in(jax.random.fold_in(rng, 6), dim), (blocks,), jnp.float32, smallest / len(cuts), largest / len(cuts))
        gain = gain * jnp.repeat(jnp.exp(steps), dims[dim] // blocks).reshape((-1,) + (1,) * (len(dims) - 1 - dim))
    return gain


def centred(rng, shape, deviation, bound, shards=(), held_as=jnp.bfloat16):
    factor_of = steps_of(rng, shape, shards, -0.22, 0.18) if shards else 1.0
    values = jax.random.normal(rng, shape, jnp.float32) * deviation * factor_of
    return jnp.minimum(jnp.maximum(values, -bound), bound).astype(held_as)


def setup_inputs(seed: int = 0) -> dict:
    arg_keys = jax.random.split(jax.random.key(seed), 13)
    return {
        "queries": draw_queries(jax.random.fold_in(arg_keys[12], 71), 0),
        "new_keys": centred(arg_keys[1], (PARTICLES, STEPS, KV_HEADS * HEAD_DIM), 1.0, 6.0, ((0, 32), (2, 8))),
        "new_values": centred(arg_keys[2], (PARTICLES, STEPS, KV_HEADS * HEAD_DIM), 1.0, 6.0, ((0, 32), (2, 8))),
        "key_cache": centred(arg_keys[3], (PARTICLES, SUFFIX, KV_HEADS * HEAD_DIM), 1.0, 6.0, ((0, 32), (2, 8))),
        "value_cache": centred(arg_keys[4], (PARTICLES, SUFFIX, KV_HEADS * HEAD_DIM), 1.0, 6.0, ((0, 32), (2, 8))),
        "prompt_keys": draw_prompt_keys(jax.random.fold_in(arg_keys[12], 71), 0),
        "prompt_values": centred(arg_keys[6], (PROMPT, KV_HEADS * HEAD_DIM), 1.0, 6.0, ((0, 32), (1, 8))),
        "lengths": draw_lengths(jax.random.fold_in(arg_keys[12], 71), 0),
        "prior": draw_prior(jax.random.fold_in(arg_keys[12], 71), 0),
        "reward_dir": centred(arg_keys[9], (HEADS * HEAD_DIM,), 1.0, 6.0, ((0, 8),), jnp.float32),
        "rungs": draw_rungs(jax.random.fold_in(arg_keys[12], 71), 0),
        "ancestors": draw_ancestors(jax.random.fold_in(arg_keys[12], 71), 0),
    }


def write_cache(cache, fresh, lengths):
    position = jnp.arange(cache.shape[1], dtype=jnp.int32)
    result = cache
    for offset in range(fresh.shape[1]):
        target = position[None, :] == (lengths[:, None] + offset)
        result = jnp.where(target[:, :, None], fresh[:, offset][:, None, :], result)
    return result


def reference(queries, new_keys, new_values, key_cache, value_cache, prompt_keys, prompt_values, lengths, prior, reward_dir, rungs, ancestors):
    groups = HEADS // KV_HEADS
    scale = HEAD_DIM ** -0.5
    blocks = PARTICLES // PART_DEV
    written_keys = write_cache(key_cache, new_keys, lengths)
    written_values = write_cache(value_cache, new_values, lengths)
    prompt_k = prompt_keys.astype(jnp.float32).reshape(PROMPT, KV_HEADS, HEAD_DIM)
    prompt_v = prompt_values.astype(jnp.float32).reshape(PROMPT, KV_HEADS, HEAD_DIM)
    position = jnp.arange(SUFFIX, dtype=jnp.int32)
    later = jnp.arange(STEPS, dtype=jnp.int32)

    def attend(inputs):
        query, cache_k, cache_v, length = inputs
        query = query.astype(jnp.float32).reshape(PART_DEV, STEPS, KV_HEADS, groups, HEAD_DIM)
        keys_four = cache_k.astype(jnp.float32).reshape(PART_DEV, SUFFIX, KV_HEADS, HEAD_DIM)
        values_four = cache_v.astype(jnp.float32).reshape(PART_DEV, SUFFIX, KV_HEADS, HEAD_DIM)
        front = jnp.einsum('psghd,ngd->psghn', query, prompt_k) * scale
        back = jnp.einsum('psghd,plgd->psghl', query, keys_four) * scale
        visible = position[None, None, :] < (length[:, None, None] + 1 + later[None, :, None])
        back = jnp.where(visible[:, :, None, None, :], back, -jnp.inf)
        peak = jnp.maximum(jnp.max(front, axis=-1), jnp.max(back, axis=-1))
        front_w = jnp.exp(front - peak[..., None])
        back_w = jnp.exp(back - peak[..., None])
        total = jnp.sum(front_w, axis=-1) + jnp.sum(back_w, axis=-1)
        front_r = lax.optimization_barrier(front_w.astype(jnp.bfloat16)).astype(jnp.float32)
        back_r = lax.optimization_barrier(back_w.astype(jnp.bfloat16)).astype(jnp.float32)
        mixed = jnp.einsum('psghn,ngd->psghd', front_r, prompt_v) + jnp.einsum('psghl,plgd->psghd', back_r, values_four)
        output = (mixed / total[..., None]).reshape(PART_DEV, STEPS, HEADS * HEAD_DIM)
        reward = jnp.sum(output * reward_dir[None, None, :], axis=-1)
        return output.astype(jnp.bfloat16), reward

    attention, rewards = lax.map(attend, (
        queries.reshape(blocks, PART_DEV, STEPS, HEADS * HEAD_DIM),
        written_keys.reshape(blocks, PART_DEV, SUFFIX, KV_HEADS * HEAD_DIM),
        written_values.reshape(blocks, PART_DEV, SUFFIX, KV_HEADS * HEAD_DIM),
        lengths.reshape(blocks, PART_DEV)))
    attention = attention.reshape(PARTICLES, STEPS, HEADS * HEAD_DIM)
    rewards = rewards.reshape(PARTICLES, STEPS)
    weights = prior + jnp.sum(rewards, axis=1)
    member = rungs[:, None] == jnp.arange(RUNGS, dtype=jnp.int32)[None, :]
    top = jnp.max(jnp.where(member, weights[:, None], -jnp.inf), axis=0)
    summed = jnp.sum(jnp.where(member, jnp.exp(weights[:, None] - top[None, :]), 0.0), axis=0)
    counted = jnp.sum(member.astype(jnp.float32), axis=0)
    rung_means = top + jnp.log(summed) - jnp.log(counted)
    next_keys = written_keys[ancestors]
    next_values = written_values[ancestors]
    next_lengths = lengths[ancestors] + STEPS
    return attention, weights, rung_means, next_keys, next_values, next_lengths
```

```python
import functools

import jax
import jax.numpy as jnp
from jax import lax
from jax.experimental import pallas as pl
from jax.experimental.pallas import tpu as pltpu
from jax.sharding import PartitionSpec as P

HEADS = 64
KV_HEADS = 8
HEAD_DIM = 128
STEPS = 2
RUNGS = 8
DISTINCT = 2
SIDES = (4, 4, 2)
WINDOW = 32
MIB = 1 << 20


def pack_kernel(lengths, rows, cache, fresh, written, packed, sems):
    count, suffix, _ = cache.shape
    written[...] = cache[...]

    def patch(p, carry):
        length = lengths[p]
        base = pl.multiple_of(jnp.minimum(length // 16 * 16, suffix - WINDOW), 16)
        block = written[p, pl.ds(base, WINDOW), :].astype(jnp.float32)
        place = lax.broadcasted_iota(jnp.int32, block.shape, 0) + base
        for offset in range(STEPS):
            line = fresh[p, pl.ds(offset, 1), :]
            block = jnp.where(place == length + offset, line, block)
        written[p, pl.ds(base, WINDOW), :] = block.astype(written.dtype)
        return carry

    lax.fori_loop(0, count, patch, 0)

    def copy(k):
        return pltpu.make_async_copy(written.at[rows[k]], packed.at[k], sems.at[k])

    def start(k, carry):
        copy(k).start()
        return carry

    def wait(k, carry):
        copy(k).wait()
        return carry

    lax.fori_loop(0, packed.shape[0], start, 0)
    lax.fori_loop(0, packed.shape[0], wait, 0)


def pack(cache, fresh, lengths, rows):
    slots = rows.shape[0]
    smem = pl.BlockSpec(memory_space=pltpu.SMEM)
    vmem = pl.BlockSpec(memory_space=pltpu.VMEM)
    return pl.pallas_call(
        pack_kernel,
        out_shape=(
            jax.ShapeDtypeStruct(cache.shape, cache.dtype),
            jax.ShapeDtypeStruct((slots,) + cache.shape[1:], cache.dtype),
        ),
        in_specs=[smem, smem, vmem, vmem],
        out_specs=(vmem, pl.BlockSpec(memory_space=pl.ANY)),
        scratch_shapes=[pltpu.SemaphoreType.DMA((slots,))],
        compiler_params=pltpu.CompilerParams(vmem_limit_bytes=24 * MIB),
        name="pack",
    )(lengths, rows, cache, fresh)


def unpack_kernel(slots, arrived, result, sems):
    def copy(p):
        return pltpu.make_async_copy(arrived.at[slots[p]], result.at[p], sems.at[p])

    def start(p, carry):
        copy(p).start()
        return carry

    def wait(p, carry):
        copy(p).wait()
        return carry

    lax.fori_loop(0, result.shape[0], start, 0)
    lax.fori_loop(0, result.shape[0], wait, 0)


def unpack(arrived, slots):
    count = slots.shape[0]
    anywhere = pl.BlockSpec(memory_space=pl.ANY)
    return pl.pallas_call(
        unpack_kernel,
        out_shape=jax.ShapeDtypeStruct((count,) + arrived.shape[1:], arrived.dtype),
        in_specs=[pl.BlockSpec(memory_space=pltpu.SMEM), anywhere],
        out_specs=anywhere,
        scratch_shapes=[pltpu.SemaphoreType.DMA((count,))],
        name="unpack",
    )(slots, arrived)


def around(array):
    sides = SIDES
    total = sides[0] * sides[1] * sides[2]
    places = [
        (i // (sides[1] * sides[2]), i // sides[2] % sides[1], i % sides[2]) for i in range(total)
    ]
    for axis in range(3):
        parts = [array]
        for step in range(1, sides[axis]):
            pairs = []
            for i, place in enumerate(places):
                goal = list(place)
                goal[axis] = (goal[axis] + step) % sides[axis]
                pairs.append((i, (goal[0] * sides[1] + goal[1]) * sides[2] + goal[2]))
            parts.append(lax.ppermute(array, "particle", pairs))
        array = jnp.concatenate(parts, axis=0)
    return array


def shards(
    queries,
    new_keys,
    new_values,
    key_cache,
    value_cache,
    prompt_keys,
    prompt_values,
    lengths,
    prior,
    reward_dir,
    rungs,
    ancestors,
):
    per_device = queries.shape[0]
    suffix = key_cache.shape[1]
    groups = HEADS // KV_HEADS
    scale = HEAD_DIM ** (-0.5)
    sources = lax.axis_size("particle")
    device = lax.axis_index("particle")

    prompt = around(jnp.stack([prompt_keys, prompt_values], axis=1))
    all_keys = prompt[:, 0]
    all_values = prompt[:, 1]

    wanted = ancestors.reshape(sources, per_device)
    owner = wanted // per_device
    local = wanted % per_device
    chosen = owner == device
    least = jnp.min(jnp.where(chosen, local, per_device - 1), axis=1)
    most = jnp.max(jnp.where(chosen, local, 0), axis=1)
    send_rows = jnp.stack([least, most], axis=1).reshape(-1)
    mine = lax.dynamic_slice_in_dim(ancestors, device * per_device, per_device)
    mine_owner = mine // per_device
    same_owner = mine_owner[:, None] == mine_owner[None, :]
    first = jnp.min(jnp.where(same_owner, mine[None, :], sources * per_device), axis=1)
    slot = mine_owner * DISTINCT + (mine != first).astype(jnp.int32)

    written_keys, outgoing_keys = pack(key_cache, new_keys.astype(jnp.float32), lengths, send_rows)
    arrived_keys = lax.all_to_all(
        outgoing_keys, "particle", split_axis=0, concat_axis=0, tiled=True
    )
    written_values, outgoing_values = pack(
        value_cache, new_values.astype(jnp.float32), lengths, send_rows
    )
    arrived_values = lax.all_to_all(
        outgoing_values, "particle", split_axis=0, concat_axis=0, tiled=True
    )
    next_keys = unpack(arrived_keys, slot)
    next_values = unpack(arrived_values, slot)

    query = queries.reshape(per_device, STEPS, groups, HEAD_DIM)
    front = (
        jnp.einsum("pshd,nd->pshn", query, all_keys, preferred_element_type=jnp.float32) * scale
    )
    back = (
        jnp.einsum("pshd,pld->pshl", query, written_keys, preferred_element_type=jnp.float32)
        * scale
    )
    position = jnp.arange(suffix, dtype=jnp.int32)
    later = jnp.arange(STEPS, dtype=jnp.int32)
    visible = position[None, None, :] < lengths[:, None, None] + 1 + later[None, :, None]
    back = jnp.where(visible[:, :, None, :], back, -jnp.inf)
    peak = jnp.maximum(jnp.max(front, axis=-1), jnp.max(back, axis=-1))
    front = jnp.exp(front - peak[..., None])
    back = jnp.exp(back - peak[..., None])
    total = jnp.sum(front, axis=-1) + jnp.sum(back, axis=-1)
    mixed = jnp.einsum(
        "pshn,nd->pshd",
        front.astype(jnp.bfloat16),
        all_values,
        preferred_element_type=jnp.float32,
    ) + jnp.einsum(
        "pshl,pld->pshd",
        back.astype(jnp.bfloat16),
        written_values,
        preferred_element_type=jnp.float32,
    )
    output = (mixed / total[..., None]).reshape(per_device, STEPS, -1)
    attention = output.astype(jnp.bfloat16)

    partial_reward = jnp.sum(output * reward_dir[None, None, :], axis=(1, 2))
    weights = prior + lax.psum(partial_reward, "tensor")
    own_rungs = lax.dynamic_slice_in_dim(rungs, device * per_device, per_device)
    ladder = jnp.arange(RUNGS, dtype=jnp.int32)
    member = own_rungs[:, None] == ladder[None, :]
    local_peak = jnp.max(jnp.where(member, weights[:, None], -1e30), axis=0)
    local_sum = jnp.sum(
        jnp.where(member, jnp.exp(weights[:, None] - local_peak[None, :]), 0.0), axis=0
    )
    shared = around(
        jnp.concatenate([local_peak, local_sum, lengths.astype(jnp.float32)])[None, :]
    )
    peaks = shared[:, :RUNGS]
    top = jnp.max(peaks, axis=0)
    summed = jnp.sum(shared[:, RUNGS : 2 * RUNGS] * jnp.exp(peaks - top[None, :]), axis=0)
    counted = jnp.sum((rungs[:, None] == ladder[None, :]).astype(jnp.float32), axis=0)
    rung_means = top + jnp.log(summed) - jnp.log(counted)

    _, wide, cores = SIDES
    tall = SIDES[0]
    up = (device // (wide * cores) - mine_owner // (wide * cores)) % tall
    along = (device // cores % wide - mine_owner // cores % wide) % wide
    across = (device % cores - mine_owner % cores) % cores
    step = (across * wide + along) * tall + up
    wanted_length = step * per_device + mine % per_device
    everywhere = shared[:, 2 * RUNGS :].reshape(-1)
    order = jnp.arange(sources * per_device, dtype=jnp.int32)
    found = jnp.sum(
        jnp.where(wanted_length[:, None] == order[None, :], everywhere[None, :], 0.0), axis=1
    )
    next_lengths = found.astype(jnp.int32) + STEPS
    return (attention, weights, rung_means, next_keys, next_values, next_lengths)


def solution(mesh):
    placed = (
        P("particle", None, "tensor"),
        P("particle", None, "tensor"),
        P("particle", None, "tensor"),
        P("particle", None, "tensor"),
        P("particle", None, "tensor"),
        P("particle", "tensor"),
        P("particle", "tensor"),
        P("particle"),
        P("particle"),
        P("tensor"),
        P(),
        P(),
    )
    return jax.shard_map(
        shards,
        mesh=mesh,
        in_specs=placed,
        out_specs=(
            P("particle", None, "tensor"),
            P("particle"),
            P(),
            P("particle", None, "tensor"),
            P("particle", None, "tensor"),
            P("particle"),
        ),
        check_vma=False,
    )
```

```python
import jax
import jax.numpy as jnp
from jax import lax
from jax.experimental import pallas as pl
from jax.experimental.pallas import tpu as pltpu
from jax.sharding import PartitionSpec as P

HEADS = 64
KV_HEADS = 8
HEAD_DIM = 128
STEPS = 2
RUNGS = 8
DISTINCT = 2
SIDES = (4, 4, 2)
WINDOW = 32


def repeat(count, body):
    def step(i, carry):
        body(i)
        return carry

    lax.fori_loop(0, count, step, 0, unroll=4)


def pack_kernel(
    lengths, least, most, cache, fresh, written, packed, held, in_sems, out_sems, low_sems, high_sems
):
    count, suffix, _ = cache.shape
    goals = least.shape[0]

    def load(p):
        return pltpu.make_async_copy(cache.at[p], held.at[p], in_sems.at[p])

    def keep(p):
        return pltpu.make_async_copy(held.at[p], written.at[p], out_sems.at[p])

    def low(d):
        return pltpu.make_async_copy(held.at[least[d]], packed.at[2 * d], low_sems.at[d])

    def high(d):
        return pltpu.make_async_copy(held.at[most[d]], packed.at[2 * d + 1], high_sems.at[d])

    def patch(p):
        load(p).wait()
        length = lengths[p]
        base = pl.multiple_of(jnp.minimum(length // 16 * 16, suffix - WINDOW), 16)
        block = held[p, pl.ds(base, WINDOW), :].astype(jnp.float32)
        lines = fresh[p].astype(jnp.float32)
        place = lax.broadcasted_iota(jnp.int32, block.shape, 0) + base
        for offset in range(STEPS):
            block = jnp.where(place == length + offset, lines[offset : offset + 1], block)
        held[p, pl.ds(base, WINDOW), :] = block.astype(held.dtype)

    repeat(count, lambda p: load(p).start())
    repeat(count, patch)
    repeat(goals, lambda d: low(d).start())
    repeat(goals, lambda d: high(d).start())
    repeat(count, lambda p: keep(p).start())
    repeat(goals, lambda d: low(d).wait())
    repeat(goals, lambda d: high(d).wait())
    repeat(count, lambda p: keep(p).wait())


def pack(cache, fresh, lengths, least, most):
    count, goals = cache.shape[0], least.shape[0]
    smem = pl.BlockSpec(memory_space=pltpu.SMEM)
    hbm = pl.BlockSpec(memory_space=pltpu.HBM)
    return pl.pallas_call(
        pack_kernel,
        out_shape=(
            jax.ShapeDtypeStruct(cache.shape, cache.dtype),
            jax.ShapeDtypeStruct((goals * DISTINCT,) + cache.shape[1:], cache.dtype),
        ),
        in_specs=[smem, smem, smem, hbm, pl.BlockSpec(memory_space=pltpu.VMEM)],
        out_specs=(hbm, hbm),
        scratch_shapes=[
            pltpu.VMEM(cache.shape, cache.dtype),
            pltpu.SemaphoreType.DMA((count,)),
            pltpu.SemaphoreType.DMA((count,)),
            pltpu.SemaphoreType.DMA((goals,)),
            pltpu.SemaphoreType.DMA((goals,)),
        ],
        name="pack",
    )(lengths, least, most, cache, fresh)


def after(array, *others):
    anywhere = pl.BlockSpec(memory_space=pl.ANY)
    return pl.pallas_call(
        lambda *refs: None,
        out_shape=jax.ShapeDtypeStruct(array.shape, array.dtype),
        in_specs=[anywhere] * (1 + len(others)),
        out_specs=anywhere,
        input_output_aliases={0: 0},
        name="after",
    )(array, *others)


def unpack_kernel(slots, arrived, _, result, held, in_sems, out_sems):
    count = result.shape[0]

    def load(p):
        return pltpu.make_async_copy(arrived.at[slots[p]], held.at[p], in_sems.at[p])

    def keep(p):
        return pltpu.make_async_copy(held.at[p], result.at[p], out_sems.at[p])

    def forward(p):
        load(p).wait()
        keep(p).start()

    repeat(count, lambda p: load(p).start())
    repeat(count, forward)
    repeat(count, lambda p: keep(p).wait())


def unpack(arrived, slots, other):
    count = slots.shape[0]
    hbm = pl.BlockSpec(memory_space=pltpu.HBM)
    shape = (count,) + arrived.shape[1:]
    return pl.pallas_call(
        unpack_kernel,
        out_shape=jax.ShapeDtypeStruct(shape, arrived.dtype),
        in_specs=[pl.BlockSpec(memory_space=pltpu.SMEM), hbm, pl.BlockSpec(memory_space=pl.ANY)],
        out_specs=hbm,
        scratch_shapes=[
            pltpu.VMEM(shape, arrived.dtype),
            pltpu.SemaphoreType.DMA((count,)),
            pltpu.SemaphoreType.DMA((count,)),
        ],
        name="unpack",
    )(slots, arrived, other)


def along(array, axis):
    sides = SIDES
    total = sides[0] * sides[1] * sides[2]
    parts = [array]
    for step in range(1, sides[axis]):
        pairs = []
        for i in range(total):
            goal = [i // (sides[1] * sides[2]), i // sides[2] % sides[1], i % sides[2]]
            goal[axis] = (goal[axis] + step) % sides[axis]
            pairs.append((i, (goal[0] * sides[1] + goal[1]) * sides[2] + goal[2]))
        parts.append(lax.ppermute(array, "particle", pairs))
    return jnp.concatenate(parts, axis=0)


def shards(
    queries,
    new_keys,
    new_values,
    key_cache,
    value_cache,
    prompt_keys,
    prompt_values,
    lengths,
    prior,
    reward_dir,
    rungs,
    ancestors,
):
    per_device = queries.shape[0]
    suffix = key_cache.shape[1]
    groups = HEADS // KV_HEADS
    scale = HEAD_DIM ** (-0.5)
    sources = lax.axis_size("particle")
    device = lax.axis_index("particle")

    plane = along(along(jnp.concatenate([prompt_keys, prompt_values], axis=1), 0), 1)
    prompt = along(plane, 2)
    all_keys = prompt[:, :HEAD_DIM]
    all_values = prompt[:, HEAD_DIM:]

    wanted = ancestors.reshape(sources, per_device)
    owner = wanted // per_device
    local = wanted % per_device
    chosen = owner == device
    least = jnp.min(jnp.where(chosen, local, per_device - 1), axis=1)
    most = jnp.max(jnp.where(chosen, local, 0), axis=1)
    mine = lax.dynamic_slice_in_dim(ancestors, device * per_device, per_device)
    mine_owner = mine // per_device
    same_owner = mine_owner[:, None] == mine_owner[None, :]
    first = jnp.min(jnp.where(same_owner, mine[None, :], sources * per_device), axis=1)
    slot = mine_owner * DISTINCT + (mine != first).astype(jnp.int32)

    written_keys, outgoing_keys = pack(key_cache, new_keys, lengths, least, most)
    arrived_keys = lax.all_to_all(
        after(outgoing_keys, plane), "particle", split_axis=0, concat_axis=0, tiled=True
    )
    written_values, outgoing_values = pack(value_cache, new_values, lengths, least, most)

    query = queries.reshape(per_device, STEPS, groups, HEAD_DIM)
    front = (
        jnp.einsum("pshd,nd->pshn", query, all_keys, preferred_element_type=jnp.float32) * scale
    )
    back = (
        jnp.einsum("pshd,pld->pshl", query, written_keys, preferred_element_type=jnp.float32)
        * scale
    )
    position = jnp.arange(suffix, dtype=jnp.int32)
    later = jnp.arange(STEPS, dtype=jnp.int32)
    visible = position[None, None, :] < lengths[:, None, None] + 1 + later[None, :, None]
    back = jnp.where(visible[:, :, None, :], back, -jnp.inf)
    peak = jnp.maximum(jnp.max(front, axis=-1), jnp.max(back, axis=-1))
    front = jnp.exp(front - peak[..., None])
    back = jnp.exp(back - peak[..., None])
    total = jnp.sum(front, axis=-1) + jnp.sum(back, axis=-1)
    mixed = jnp.einsum(
        "pshn,nd->pshd",
        front.astype(jnp.bfloat16),
        all_values,
        preferred_element_type=jnp.float32,
    ) + jnp.einsum(
        "pshl,pld->pshd",
        back.astype(jnp.bfloat16),
        written_values,
        preferred_element_type=jnp.float32,
    )
    output = (mixed / total[..., None]).reshape(per_device, STEPS, -1)
    attention = output.astype(jnp.bfloat16)

    partial_reward = jnp.sum(output * reward_dir[None, None, :], axis=(1, 2))
    weights = prior + lax.psum(partial_reward, "tensor")
    own_rungs = lax.dynamic_slice_in_dim(rungs, device * per_device, per_device)
    ladder = jnp.arange(RUNGS, dtype=jnp.int32)
    member = own_rungs[:, None] == ladder[None, :]
    local_peak = jnp.max(jnp.where(member, weights[:, None], -1e30), axis=0)
    local_sum = jnp.sum(
        jnp.where(member, jnp.exp(weights[:, None] - local_peak[None, :]), 0.0), axis=0
    )
    shared = jnp.concatenate([local_peak, local_sum, lengths.astype(jnp.float32)])[None, :]
    near = along(along(shared, 2), 0)
    arrived_values = lax.all_to_all(
        after(outgoing_values, near), "particle", split_axis=0, concat_axis=0, tiled=True
    )
    next_keys = unpack(arrived_keys, slot, near)
    shared = along(after(near, next_keys), 1)
    peaks = shared[:, :RUNGS]
    top = jnp.max(peaks, axis=0)
    summed = jnp.sum(shared[:, RUNGS : 2 * RUNGS] * jnp.exp(peaks - top[None, :]), axis=0)
    counted = jnp.sum((rungs[:, None] == ladder[None, :]).astype(jnp.float32), axis=0)
    rung_means = top + jnp.log(summed) - jnp.log(counted)

    tall, wide, cores = SIDES
    up = (device // (wide * cores) - mine_owner // (wide * cores)) % tall
    right = (device // cores % wide - mine_owner // cores % wide) % wide
    across = (device % cores - mine_owner % cores) % cores
    step = (right * tall + up) * cores + across
    wanted_length = step * per_device + mine % per_device
    everywhere = shared[:, 2 * RUNGS :].reshape(-1)
    order = jnp.arange(sources * per_device, dtype=jnp.int32)
    found = jnp.sum(
        jnp.where(wanted_length[:, None] == order[None, :], everywhere[None, :], 0.0), axis=1
    )
    next_lengths = found.astype(jnp.int32) + STEPS
    next_values = unpack(arrived_values, slot, shared)
    return (attention, weights, rung_means, next_keys, next_values, next_lengths)


def solution(mesh):
    placed = (
        P("particle", None, "tensor"),
        P("particle", None, "tensor"),
        P("particle", None, "tensor"),
        P("particle", None, "tensor"),
        P("particle", None, "tensor"),
        P("particle", "tensor"),
        P("particle", "tensor"),
        P("particle"),
        P("particle"),
        P("tensor"),
        P(),
        P(),
    )
    return jax.shard_map(
        shards,
        mesh=mesh,
        in_specs=placed,
        out_specs=(
            P("particle", None, "tensor"),
            P("particle"),
            P(),
            P("particle", None, "tensor"),
            P("particle", None, "tensor"),
            P("particle"),
        ),
        check_vma=False,
    )
```

```python
import itertools

import jax
import jax.numpy as jnp
from jax import lax
from jax.experimental import pallas as pl
from jax.experimental.pallas import tpu as pltpu
from jax.sharding import PartitionSpec as P

HEADS = 64
KV_HEADS = 8
HEAD_DIM = 128
STEPS = 2
RUNGS = 8
DISTINCT = 2
SIDES = (4, 4, 2)
WINDOW = 32
CHUNKS = 4
GROUP = 2
ROOMY = 58 << 20


def repeat(count, body):
    def step(i, carry):
        body(i)
        return carry

    lax.fori_loop(0, count, step, 0, unroll=4)


def pack_kernel(
    lengths,
    least,
    most,
    keys,
    values,
    new_keys,
    new_values,
    packed,
    written_keys,
    written_values,
    held,
    in_sems,
    out_sems,
    low_sems,
    high_sems,
):
    count, suffix, _ = keys.shape
    goals = least.shape[0]
    share = count // CHUNKS
    parts = ((keys, new_keys, written_keys), (values, new_values, written_values))

    def load(chunk, half):
        rows = pl.ds(chunk * share, share)
        return pltpu.make_async_copy(
            parts[half][0].at[rows],
            held.at[rows, pl.ds(half * suffix, suffix)],
            in_sems.at[chunk * 2 + half],
        )

    def keep(half):
        return pltpu.make_async_copy(
            held.at[:, pl.ds(half * suffix, suffix)], parts[half][2], out_sems.at[half]
        )

    def low(d):
        return pltpu.make_async_copy(held.at[least[d]], packed.at[2 * d], low_sems.at[d])

    def high(d):
        return pltpu.make_async_copy(held.at[most[d]], packed.at[2 * d + 1], high_sems.at[d])

    def patch(group):
        found = []
        for i in range(GROUP):
            p = group * GROUP + i
            length = lengths[p]
            base = pl.multiple_of(jnp.minimum(length // 16 * 16, suffix - WINDOW), 16)
            for half in range(2):
                place = (p, pl.ds(base + half * suffix, WINDOW))
                block = held[place].astype(jnp.float32)
                lines = parts[half][1][p].astype(jnp.float32)
                row = lax.broadcasted_iota(jnp.int32, block.shape, 0) + base
                for offset in range(STEPS):
                    block = jnp.where(row == length + offset, lines[offset : offset + 1], block)
                found.append((place, block.astype(held.dtype)))
        for place, block in found:
            held[place] = block

    for chunk in range(CHUNKS):
        for half in range(2):
            load(chunk, half).start()
    for chunk in range(CHUNKS):
        for half in range(2):
            load(chunk, half).wait()
        repeat(share // GROUP, lambda g, chunk=chunk: patch(g + chunk * (share // GROUP)), 1)
    repeat(goals, lambda d: low(d).start())
    repeat(goals, lambda d: high(d).start())
    keep(0).start()
    keep(1).start()
    repeat(goals, lambda d: low(d).wait())
    repeat(goals, lambda d: high(d).wait())
    keep(0).wait()
    keep(1).wait()


def repeat(count, body, unroll=4):
    def step(i, carry):
        body(i)
        return carry

    lax.fori_loop(0, count, step, 0, unroll=unroll)


def pack(keys, values, new_keys, new_values, lengths, least, most):
    (count, suffix, width), goals = keys.shape, least.shape[0]
    smem = pl.BlockSpec(memory_space=pltpu.SMEM)
    hbm = pl.BlockSpec(memory_space=pltpu.HBM)
    vmem = pl.BlockSpec(memory_space=pltpu.VMEM)
    return pl.pallas_call(
        pack_kernel,
        out_shape=(
            jax.ShapeDtypeStruct((goals * DISTINCT, 2 * suffix, width), keys.dtype),
            jax.ShapeDtypeStruct(keys.shape, keys.dtype),
            jax.ShapeDtypeStruct(values.shape, values.dtype),
        ),
        in_specs=[smem, smem, smem, hbm, hbm, vmem, vmem],
        out_specs=(hbm, hbm, hbm),
        scratch_shapes=[
            pltpu.VMEM((count, 2 * suffix, width), keys.dtype),
            pltpu.SemaphoreType.DMA((2 * CHUNKS,)),
            pltpu.SemaphoreType.DMA((2,)),
            pltpu.SemaphoreType.DMA((goals,)),
            pltpu.SemaphoreType.DMA((goals,)),
        ],
        name="pack",
    )(lengths, least, most, keys, values, new_keys, new_values)


def after(array, *others):
    hbm = pl.BlockSpec(memory_space=pltpu.HBM)
    return pl.pallas_call(
        lambda *refs: None,
        out_shape=jax.ShapeDtypeStruct(array.shape, array.dtype),
        in_specs=[hbm] + [pl.BlockSpec(memory_space=pl.ANY)] * len(others),
        out_specs=hbm,
        input_output_aliases={0: 0},
        compiler_params=pltpu.CompilerParams(vmem_limit_bytes=ROOMY),
        name="after",
    )(array, *others)


def unpack_kernel(slots, arrived, _, next_keys, next_values, mark, held, in_sems, out_sems):
    count, suffix, _ = next_keys.shape
    share = count // CHUNKS

    def load(p):
        return pltpu.make_async_copy(arrived.at[slots[p]], held.at[p], in_sems.at[p])

    def keep(chunk, half):
        rows = pl.ds(chunk * share, share)
        return pltpu.make_async_copy(
            held.at[rows, pl.ds(half * suffix, suffix)],
            (next_keys, next_values)[half].at[rows],
            out_sems.at[chunk * 2 + half],
        )

    mark[...] = jnp.zeros_like(mark)
    repeat(count, lambda p: load(p).start())
    for chunk in range(CHUNKS):
        repeat(share, lambda p, chunk=chunk: load(p + chunk * share).wait())
        for half in range(2):
            keep(chunk, half).start()
    for chunk in range(CHUNKS):
        for half in range(2):
            keep(chunk, half).wait()


def unpack(arrived, slots, other):
    count, (_, length, width) = slots.shape[0], arrived.shape
    hbm = pl.BlockSpec(memory_space=pltpu.HBM)
    shape = jax.ShapeDtypeStruct((count, length // 2, width), arrived.dtype)
    return pl.pallas_call(
        unpack_kernel,
        out_shape=(shape, shape, jax.ShapeDtypeStruct((1, width), jnp.float32)),
        in_specs=[pl.BlockSpec(memory_space=pltpu.SMEM), hbm, pl.BlockSpec(memory_space=pl.ANY)],
        out_specs=(hbm, hbm, pl.BlockSpec(memory_space=pltpu.VMEM)),
        scratch_shapes=[
            pltpu.VMEM((count, length, width), arrived.dtype),
            pltpu.SemaphoreType.DMA((count,)),
            pltpu.SemaphoreType.DMA((2 * CHUNKS,)),
        ],
        name="unpack",
    )(slots, arrived, other)


def finish_kernel(counted, step, place, *refs):
    *parts, _, rung_means, next_lengths = refs
    shared = jnp.concatenate([part[...] for part in parts], axis=0)
    peaks, sums, filled = shared[:, 0], shared[:, 1], shared[:, 2]
    top = jnp.max(peaks, axis=0, keepdims=True)
    summed = jnp.sum(sums * jnp.exp(peaks - top), axis=0, keepdims=True)
    rung_means[...] = top + jnp.log(summed) - jnp.log(counted[...])
    order = lax.broadcasted_iota(jnp.int32, filled.shape, 0)
    owner = (order == step[...]).astype(jnp.float32)
    found = lax.dot_general(
        filled, owner, (((0,), (0,)), ((), ())), preferred_element_type=jnp.float32
    )
    order = lax.broadcasted_iota(jnp.int32, found.shape, 0)
    length = jnp.sum(jnp.where(order == place[...], found, 0.0), axis=0, keepdims=True)
    next_lengths[...] = length.astype(jnp.int32) + STEPS


def finish(parts, counted, step, place, other):
    vmem = pl.BlockSpec(memory_space=pltpu.VMEM)
    row = (1, step.shape[1])
    return pl.pallas_call(
        finish_kernel,
        out_shape=(
            jax.ShapeDtypeStruct(row, jnp.float32),
            jax.ShapeDtypeStruct(row, jnp.int32),
        ),
        in_specs=[vmem] * (3 + len(parts)) + [pl.BlockSpec(memory_space=pl.ANY)],
        out_specs=(vmem, vmem),
        compiler_params=pltpu.CompilerParams(vmem_limit_bytes=ROOMY),
        name="finish",
    )(counted, step, place, *parts, other)


def along(array, axes):
    sides = SIDES
    total = sides[0] * sides[1] * sides[2]
    parts = []
    for steps in itertools.product(*(range(sides[axis]) for axis in axes)):
        pairs = []
        for i in range(total):
            goal = [i // (sides[1] * sides[2]), i // sides[2] % sides[1], i % sides[2]]
            for axis, step in zip(axes, steps):
                goal[axis] = (goal[axis] + step) % sides[axis]
            pairs.append((i, (goal[0] * sides[1] + goal[1]) * sides[2] + goal[2]))
        parts.append(lax.ppermute(array, "particle", pairs) if any(steps) else array)
    return parts


def shards(
    queries,
    new_keys,
    new_values,
    key_cache,
    value_cache,
    prompt_keys,
    prompt_values,
    lengths,
    prior,
    reward_dir,
    rungs,
    ancestors,
):
    per_device = queries.shape[0]
    suffix = key_cache.shape[1]
    groups = HEADS // KV_HEADS
    scale = HEAD_DIM ** (-0.5)
    sources = lax.axis_size("particle")
    device = lax.axis_index("particle")

    shard = jnp.concatenate([prompt_keys, prompt_values], axis=1)
    column = jnp.concatenate(along(shard, (0,)), axis=0)
    columns = along(column, (1,))
    prompt = jnp.concatenate(along(jnp.concatenate(columns, axis=0), (2,)), axis=0)
    all_keys = prompt[:, :HEAD_DIM]
    all_values = prompt[:, HEAD_DIM:]

    wanted = ancestors.reshape(sources, per_device)
    owner = wanted // per_device
    local = wanted % per_device
    chosen = owner == device
    least = jnp.min(jnp.where(chosen, local, per_device - 1), axis=1)
    most = jnp.max(jnp.where(chosen, local, 0), axis=1)
    mine = lax.dynamic_slice_in_dim(ancestors, device * per_device, per_device)
    mine_owner = mine // per_device
    same_owner = mine_owner[:, None] == mine_owner[None, :]
    first = jnp.min(jnp.where(same_owner, mine[None, :], sources * per_device), axis=1)
    slot = mine_owner * DISTINCT + (mine != first).astype(jnp.int32)

    outgoing, written_keys, written_values = pack(
        key_cache, value_cache, new_keys, new_values, lengths, least, most
    )
    arrived = lax.all_to_all(
        after(outgoing, *columns[1:]), "particle", split_axis=0, concat_axis=0, tiled=True
    )

    query = queries.reshape(per_device, STEPS, groups, HEAD_DIM)
    front = (
        jnp.einsum("pshd,nd->pshn", query, all_keys, preferred_element_type=jnp.float32) * scale
    )
    back = (
        jnp.einsum("pshd,pld->pshl", query, written_keys, preferred_element_type=jnp.float32)
        * scale
    )
    position = jnp.arange(suffix, dtype=jnp.int32)
    later = jnp.arange(STEPS, dtype=jnp.int32)
    visible = position[None, None, :] < lengths[:, None, None] + 1 + later[None, :, None]
    back = jnp.where(visible[:, :, None, :], back, -jnp.inf)
    peak = jnp.maximum(jnp.max(front, axis=-1), jnp.max(back, axis=-1))
    front = jnp.exp(front - peak[..., None])
    back = jnp.exp(back - peak[..., None])
    total = jnp.sum(front, axis=-1) + jnp.sum(back, axis=-1)
    mixed = jnp.einsum(
        "pshn,nd->pshd",
        front.astype(jnp.bfloat16),
        all_values,
        preferred_element_type=jnp.float32,
    ) + jnp.einsum(
        "pshl,pld->pshd",
        back.astype(jnp.bfloat16),
        written_values,
        preferred_element_type=jnp.float32,
    )
    output = (mixed / total[..., None]).reshape(per_device, STEPS, -1)
    attention = output.astype(jnp.bfloat16)

    partial_reward = jnp.sum(output * reward_dir[None, None, :], axis=(1, 2))
    weights = prior + lax.psum(partial_reward, "tensor")
    own_rungs = lax.dynamic_slice_in_dim(rungs, device * per_device, per_device)
    ladder = jnp.arange(RUNGS, dtype=jnp.int32)
    member = own_rungs[:, None] == ladder[None, :]
    local_peak = jnp.max(jnp.where(member, weights[:, None], -1e30), axis=0)
    local_sum = jnp.sum(
        jnp.where(member, jnp.exp(weights[:, None] - local_peak[None, :]), 0.0), axis=0
    )
    spare = per_device - RUNGS
    shared = jnp.stack(
        [
            jnp.pad(local_peak, (0, spare)),
            jnp.pad(local_sum, (0, spare), constant_values=1.0),
            lengths.astype(jnp.float32),
        ]
    )[None]
    near = jnp.concatenate(along(shared, (2,)), axis=0)
    near = jnp.concatenate(along(near, (0,)), axis=0)
    parts = along(near, (1,))
    next_keys, next_values, mark = unpack(arrived, slot, near)

    counted = jnp.sum((rungs[:, None] == ladder[None, :]).astype(jnp.float32), axis=0)
    tall, wide, cores = SIDES
    up = (device // (wide * cores) - mine_owner // (wide * cores)) % tall
    right = (device // cores % wide - mine_owner // cores % wide) % wide
    across = (device % cores - mine_owner % cores) % cores
    step = (right * tall + up) * cores + across
    rung_means, next_lengths = finish(
        parts,
        jnp.pad(counted, (0, spare), constant_values=1.0)[None],
        step[None],
        (mine % per_device)[None],
        mark,
    )
    rung_means = rung_means[0, :RUNGS]
    next_lengths = next_lengths[0]
    return (attention, weights, rung_means, next_keys, next_values, next_lengths)


def solution(mesh):
    placed = (
        P("particle", None, "tensor"),
        P("particle", None, "tensor"),
        P("particle", None, "tensor"),
        P("particle", None, "tensor"),
        P("particle", None, "tensor"),
        P("particle", "tensor"),
        P("particle", "tensor"),
        P("particle"),
        P("particle"),
        P("tensor"),
        P(),
        P(),
    )
    return jax.shard_map(
        shards,
        mesh=mesh,
        in_specs=placed,
        out_specs=(
            P("particle", None, "tensor"),
            P("particle"),
            P(),
            P("particle", None, "tensor"),
            P("particle", None, "tensor"),
            P("particle"),
        ),
        check_vma=False,
    )
```

```python
import functools
import itertools

import jax
import jax.numpy as jnp
from jax import lax
from jax.experimental import pallas as pl
from jax.experimental.pallas import tpu as pltpu
from jax.sharding import PartitionSpec as P

HEADS = 64
KV_HEADS = 8
HEAD_DIM = 128
STEPS = 2
RUNGS = 8
DISTINCT = 2
SIDES = (4, 4, 2)
WINDOW = 32
CHUNKS = 4
GROUP = 2
ROOMY = 58 << 20


def repeat(count, body):
    def step(i, carry):
        body(i)
        return carry

    lax.fori_loop(0, count, step, 0, unroll=4)


def pack_kernel(keeps, lengths, least, most, *refs):
    number = (len(refs) - 5) // (2 + keeps)
    caches, fresh, (packed, *written) = refs[:number], refs[number : 2 * number], refs[2 * number : -4]
    held, in_sems, out_sems, send_sems = refs[-4:]
    count, suffix, _ = caches[0].shape
    goals = least.shape[0]
    share = count // CHUNKS

    def load(chunk, n):
        rows = pl.ds(chunk * share, share)
        return pltpu.make_async_copy(
            caches[n].at[rows], held.at[n, rows], in_sems.at[chunk * number + n]
        )

    def keep(n):
        return pltpu.make_async_copy(held.at[n], written[n], out_sems.at[n])

    def low(d):
        return pltpu.make_async_copy(
            held.at[number - 1, least[d]], packed.at[2 * d], send_sems.at[2 * d]
        )

    def high(d):
        return pltpu.make_async_copy(
            held.at[number - 1, most[d]], packed.at[2 * d + 1], send_sems.at[2 * d + 1]
        )

    def patch(group):
        found = []
        for i in range(GROUP):
            p = group * GROUP + i
            length = lengths[p]
            base = pl.multiple_of(jnp.minimum(length // 16 * 16, suffix - WINDOW), 16)
            for n in range(number):
                place = (n, p, pl.ds(base, WINDOW))
                block = held[place].astype(jnp.float32)
                lines = fresh[n][p].astype(jnp.float32)
                row = lax.broadcasted_iota(jnp.int32, block.shape, 0) + base
                for offset in range(STEPS):
                    block = jnp.where(row == length + offset, lines[offset : offset + 1], block)
                found.append((place, block.astype(held.dtype)))
        for place, block in found:
            held[place] = block

    for chunk in range(CHUNKS):
        for n in range(number):
            load(chunk, n).start()
    for chunk in range(CHUNKS):
        for n in range(number):
            load(chunk, n).wait()
        groups = share // GROUP
        repeat(groups, lambda g, chunk=chunk: patch(g + chunk * groups), 1)
    repeat(goals, lambda d: (low(d).start(), high(d).start()))
    for n in range(number * keeps):
        keep(n).start()
    repeat(goals, lambda d: (low(d).wait(), high(d).wait()))
    for n in range(number * keeps):
        keep(n).wait()


def repeat(count, body, unroll=4):
    def step(i, carry):
        body(i)
        return carry

    lax.fori_loop(0, count, step, 0, unroll=unroll)


def pack(caches, fresh, lengths, least, most, keeps):
    cache, number = caches[0], len(caches)
    count, goals = cache.shape[0], least.shape[0]
    smem = pl.BlockSpec(memory_space=pltpu.SMEM)
    hbm = pl.BlockSpec(memory_space=pltpu.HBM)
    vmem = pl.BlockSpec(memory_space=pltpu.VMEM)
    return pl.pallas_call(
        functools.partial(pack_kernel, keeps),
        out_shape=[jax.ShapeDtypeStruct((goals * DISTINCT,) + cache.shape[1:], cache.dtype)]
        + [jax.ShapeDtypeStruct(cache.shape, cache.dtype)] * (number * keeps),
        in_specs=[smem] * 3 + [hbm] * number + [vmem] * number,
        out_specs=[hbm] * (1 + number * keeps),
        scratch_shapes=[
            pltpu.VMEM((number,) + cache.shape, cache.dtype),
            pltpu.SemaphoreType.DMA((number * CHUNKS,)),
            pltpu.SemaphoreType.DMA((number,)),
            pltpu.SemaphoreType.DMA((goals * DISTINCT,)),
        ],
        name="pack",
    )(lengths, least, most, *caches, *fresh)


def after(array, *others):
    hbm = pl.BlockSpec(memory_space=pltpu.HBM)
    return pl.pallas_call(
        lambda *refs: None,
        out_shape=jax.ShapeDtypeStruct(array.shape, array.dtype),
        in_specs=[hbm] + [pl.BlockSpec(memory_space=pl.ANY)] * len(others),
        out_specs=hbm,
        input_output_aliases={0: 0},
        compiler_params=pltpu.CompilerParams(vmem_limit_bytes=ROOMY),
        name="after",
    )(array, *others)


def unpack_kernel(slots, arrived, _, result, mark, held, in_sems, out_sems):
    count = result.shape[0]
    share = count // CHUNKS

    def load(p):
        return pltpu.make_async_copy(arrived.at[slots[p]], held.at[p], in_sems.at[p])

    def keep(chunk):
        rows = pl.ds(chunk * share, share)
        return pltpu.make_async_copy(held.at[rows], result.at[rows], out_sems.at[chunk])

    mark[...] = jnp.zeros_like(mark)
    repeat(count, lambda p: load(p).start())
    for chunk in range(CHUNKS):
        repeat(share, lambda p, chunk=chunk: load(p + chunk * share).wait())
        keep(chunk).start()
    for chunk in range(CHUNKS):
        keep(chunk).wait()


def unpack(arrived, slots, other):
    count, (_, suffix, width) = slots.shape[0], arrived.shape
    hbm = pl.BlockSpec(memory_space=pltpu.HBM)
    shape = (count, suffix, width)
    return pl.pallas_call(
        unpack_kernel,
        out_shape=(
            jax.ShapeDtypeStruct(shape, arrived.dtype),
            jax.ShapeDtypeStruct((1, width), jnp.float32),
        ),
        in_specs=[pl.BlockSpec(memory_space=pltpu.SMEM), hbm, pl.BlockSpec(memory_space=pl.ANY)],
        out_specs=(hbm, pl.BlockSpec(memory_space=pltpu.VMEM)),
        scratch_shapes=[
            pltpu.VMEM(shape, arrived.dtype),
            pltpu.SemaphoreType.DMA((count,)),
            pltpu.SemaphoreType.DMA((CHUNKS,)),
        ],
        name="unpack",
    )(slots, arrived, other)


def finish_kernel(counted, step, place, *refs):
    *parts, _, rung_means, next_lengths = refs
    shared = jnp.concatenate([part[...] for part in parts], axis=0)
    peaks, sums, filled = shared[:, 0], shared[:, 1], shared[:, 2]
    top = jnp.max(peaks, axis=0, keepdims=True)
    summed = jnp.sum(sums * jnp.exp(peaks - top), axis=0, keepdims=True)
    rung_means[...] = (top + jnp.log(summed) - jnp.log(counted[...]))[:, :RUNGS]
    order = lax.broadcasted_iota(jnp.int32, filled.shape, 0)
    owner = (order == step[...]).astype(jnp.float32)
    found = lax.dot_general(
        filled, owner, (((0,), (0,)), ((), ())), preferred_element_type=jnp.float32
    )
    order = lax.broadcasted_iota(jnp.int32, found.shape, 0)
    length = jnp.sum(jnp.where(order == place[...], found, 0.0), axis=0, keepdims=True)
    next_lengths[...] = length.astype(jnp.int32) + STEPS


def finish(parts, counted, step, place, other):
    vmem = pl.BlockSpec(memory_space=pltpu.VMEM)
    return pl.pallas_call(
        finish_kernel,
        out_shape=(
            jax.ShapeDtypeStruct((1, RUNGS), jnp.float32),
            jax.ShapeDtypeStruct(step.shape, jnp.int32),
        ),
        in_specs=[vmem] * (3 + len(parts)) + [pl.BlockSpec(memory_space=pl.ANY)],
        out_specs=(vmem, vmem),
        compiler_params=pltpu.CompilerParams(vmem_limit_bytes=ROOMY),
        name="finish",
    )(counted, step, place, *parts, other)


def along(array, axes):
    sides = SIDES
    total = sides[0] * sides[1] * sides[2]
    parts = []
    for steps in itertools.product(*(range(sides[axis]) for axis in axes)):
        pairs = []
        for i in range(total):
            goal = [i // (sides[1] * sides[2]), i // sides[2] % sides[1], i % sides[2]]
            for axis, step in zip(axes, steps):
                goal[axis] = (goal[axis] + step) % sides[axis]
            pairs.append((i, (goal[0] * sides[1] + goal[1]) * sides[2] + goal[2]))
        parts.append(lax.ppermute(array, "particle", pairs) if any(steps) else array)
    return parts


def shards(
    queries,
    new_keys,
    new_values,
    key_cache,
    value_cache,
    prompt_keys,
    prompt_values,
    lengths,
    prior,
    reward_dir,
    rungs,
    ancestors,
):
    per_device = queries.shape[0]
    suffix = key_cache.shape[1]
    groups = HEADS // KV_HEADS
    scale = HEAD_DIM ** (-0.5)
    sources = lax.axis_size("particle")
    device = lax.axis_index("particle")

    shard = jnp.concatenate([prompt_keys, prompt_values], axis=1)
    column = jnp.concatenate(along(shard, (0,)), axis=0)
    plane = jnp.concatenate(along(column, (1,)), axis=0)
    prompt = jnp.concatenate(along(plane, (2,)), axis=0)
    all_keys = prompt[:, :HEAD_DIM]
    all_values = prompt[:, HEAD_DIM:]

    wanted = ancestors.reshape(sources, per_device)
    owner = wanted // per_device
    local = wanted % per_device
    chosen = owner == device
    least = jnp.min(jnp.where(chosen, local, per_device - 1), axis=1)
    most = jnp.max(jnp.where(chosen, local, 0), axis=1)
    mine = lax.dynamic_slice_in_dim(ancestors, device * per_device, per_device)
    mine_owner = mine // per_device
    same_owner = mine_owner[:, None] == mine_owner[None, :]
    first = jnp.min(jnp.where(same_owner, mine[None, :], sources * per_device), axis=1)
    slot = mine_owner * DISTINCT + (mine != first).astype(jnp.int32)

    exchange = functools.partial(
        lax.all_to_all, axis_name="particle", split_axis=0, concat_axis=0, tiled=True
    )
    places = (lengths, least, most)
    (outgoing_keys,) = pack((key_cache,), (new_keys,), *places, False)
    arrived_keys = exchange(after(outgoing_keys, column))
    outgoing_values, written_keys, written_values = pack(
        (key_cache, value_cache), (new_keys, new_values), *places, True
    )
    arrived_values = exchange(after(outgoing_values, arrived_keys))
    next_keys, mark = unpack(arrived_keys, slot, column)

    query = queries.reshape(per_device, STEPS, groups, HEAD_DIM)
    front = (
        jnp.einsum("pshd,nd->pshn", query, all_keys, preferred_element_type=jnp.float32) * scale
    )
    back = (
        jnp.einsum("pshd,pld->pshl", query, written_keys, preferred_element_type=jnp.float32)
        * scale
    )
    position = jnp.arange(suffix, dtype=jnp.int32)
    later = jnp.arange(STEPS, dtype=jnp.int32)
    visible = position[None, None, :] < lengths[:, None, None] + 1 + later[None, :, None]
    back = jnp.where(visible[:, :, None, :], back, -jnp.inf)
    peak = jnp.maximum(jnp.max(front, axis=-1), jnp.max(back, axis=-1))
    front = jnp.exp(front - peak[..., None])
    back = jnp.exp(back - peak[..., None])
    total = jnp.sum(front, axis=-1) + jnp.sum(back, axis=-1)
    mixed = jnp.einsum(
        "pshn,nd->pshd",
        front.astype(jnp.bfloat16),
        all_values,
        preferred_element_type=jnp.float32,
    ) + jnp.einsum(
        "pshl,pld->pshd",
        back.astype(jnp.bfloat16),
        written_values,
        preferred_element_type=jnp.float32,
    )
    output = (mixed / total[..., None]).reshape(per_device, STEPS, -1)
    attention = output.astype(jnp.bfloat16)

    partial_reward = jnp.sum(output * reward_dir[None, None, :], axis=(1, 2))
    weights = prior + lax.psum(partial_reward, "tensor")
    own_rungs = lax.dynamic_slice_in_dim(rungs, device * per_device, per_device)
    ladder = jnp.arange(RUNGS, dtype=jnp.int32)
    member = own_rungs[:, None] == ladder[None, :]
    local_peak = jnp.max(jnp.where(member, weights[:, None], -1e30), axis=0)
    local_sum = jnp.sum(
        jnp.where(member, jnp.exp(weights[:, None] - local_peak[None, :]), 0.0), axis=0
    )
    spare = per_device - RUNGS
    shared = jnp.stack(
        [
            jnp.pad(local_peak, (0, spare)),
            jnp.pad(local_sum, (0, spare), constant_values=1.0),
            lengths.astype(jnp.float32) + mark[0, :per_device],
        ]
    )[None]
    near = jnp.concatenate(along(shared, (2,)), axis=0)
    near = jnp.concatenate(along(near, (0,)), axis=0)
    parts = along(near, (1,))
    next_values, mark = unpack(arrived_values, slot, near)

    counted = jnp.sum((rungs[:, None] == ladder[None, :]).astype(jnp.float32), axis=0)
    tall, wide, cores = SIDES
    up = (device // (wide * cores) - mine_owner // (wide * cores)) % tall
    right = (device // cores % wide - mine_owner // cores % wide) % wide
    across = (device % cores - mine_owner % cores) % cores
    step = (right * tall + up) * cores + across
    rung_means, next_lengths = finish(
        parts,
        jnp.pad(counted, (0, spare), constant_values=1.0)[None],
        step[None],
        (mine % per_device)[None],
        mark,
    )
    rung_means = rung_means[0]
    next_lengths = next_lengths[0]
    return (attention, weights, rung_means, next_keys, next_values, next_lengths)


def solution(mesh):
    placed = (
        P("particle", None, "tensor"),
        P("particle", None, "tensor"),
        P("particle", None, "tensor"),
        P("particle", None, "tensor"),
        P("particle", None, "tensor"),
        P("particle", "tensor"),
        P("particle", "tensor"),
        P("particle"),
        P("particle"),
        P("tensor"),
        P(),
        P(),
    )
    return jax.shard_map(
        shards,
        mesh=mesh,
        in_specs=placed,
        out_specs=(
            P("particle", None, "tensor"),
            P("particle"),
            P(),
            P("particle", None, "tensor"),
            P("particle", None, "tensor"),
            P("particle"),
        ),
        check_vma=False,
    )
```

```python
import functools
import itertools

import jax
import jax.numpy as jnp
from jax import lax
from jax.experimental import pallas as pl
from jax.experimental.pallas import tpu as pltpu
from jax.sharding import PartitionSpec as P

HEADS = 64
KV_HEADS = 8
HEAD_DIM = 128
STEPS = 2
RUNGS = 8
DISTINCT = 2
SIDES = (4, 4, 2)
PLANES = 8
WINDOW = 32
CHUNKS = 4
GROUP = 2
ROOMY = 58 << 20


def pack_kernel(keeps, lengths, least, most, *refs):
    number = (len(refs) - 5) // (2 + keeps)
    caches, fresh, (packed, *written) = refs[:number], refs[number : 2 * number], refs[2 * number : -4]
    held, in_sems, out_sems, send_sems = refs[-4:]
    count, suffix, _ = caches[0].shape
    goals = least.shape[0]
    share = count // CHUNKS

    def load(chunk, n):
        rows = pl.ds(chunk * share, share)
        return pltpu.make_async_copy(
            caches[n].at[rows], held.at[n, rows], in_sems.at[chunk * number + n]
        )

    def keep(n):
        return pltpu.make_async_copy(held.at[n], written[n], out_sems.at[n])

    def low(d):
        return pltpu.make_async_copy(
            held.at[number - 1, least[d]], packed.at[2 * d], send_sems.at[2 * d]
        )

    def high(d):
        return pltpu.make_async_copy(
            held.at[number - 1, most[d]], packed.at[2 * d + 1], send_sems.at[2 * d + 1]
        )

    def patch(group):
        found = []
        for i in range(GROUP):
            p = group * GROUP + i
            length = lengths[p]
            base = pl.multiple_of(jnp.minimum(length // 16 * 16, suffix - WINDOW), 16)
            for n in range(number):
                place = (n, p, pl.ds(base, WINDOW))
                block = held[place].astype(jnp.float32)
                lines = fresh[n][p].astype(jnp.float32)
                row = lax.broadcasted_iota(jnp.int32, block.shape, 0) + base
                for offset in range(STEPS):
                    block = jnp.where(row == length + offset, lines[offset : offset + 1], block)
                found.append((place, block.astype(held.dtype)))
        for place, block in found:
            held[place] = block

    for chunk in range(CHUNKS):
        for n in range(number):
            load(chunk, n).start()
    for chunk in range(CHUNKS):
        for n in range(number):
            load(chunk, n).wait()
        groups = share // GROUP
        repeat(groups, lambda g, chunk=chunk: patch(g + chunk * groups), 1)
    repeat(goals, lambda d: (low(d).start(), high(d).start()))
    for n in range(number * keeps):
        keep(n).start()
    repeat(goals, lambda d: (low(d).wait(), high(d).wait()))
    for n in range(number * keeps):
        keep(n).wait()


def repeat(count, body, unroll=4):
    def step(i, carry):
        body(i)
        return carry

    lax.fori_loop(0, count, step, 0, unroll=unroll)


def pack(caches, fresh, lengths, least, most, keeps):
    cache, number = caches[0], len(caches)
    count, goals = cache.shape[0], least.shape[0]
    smem = pl.BlockSpec(memory_space=pltpu.SMEM)
    hbm = pl.BlockSpec(memory_space=pltpu.HBM)
    vmem = pl.BlockSpec(memory_space=pltpu.VMEM)
    return pl.pallas_call(
        functools.partial(pack_kernel, keeps),
        out_shape=[jax.ShapeDtypeStruct((goals * DISTINCT,) + cache.shape[1:], cache.dtype)]
        + [jax.ShapeDtypeStruct(cache.shape, cache.dtype)] * (number * keeps),
        in_specs=[smem] * 3 + [hbm] * number + [vmem] * number,
        out_specs=[hbm] * (1 + number * keeps),
        scratch_shapes=[
            pltpu.VMEM((number,) + cache.shape, cache.dtype),
            pltpu.SemaphoreType.DMA((number * CHUNKS,)),
            pltpu.SemaphoreType.DMA((number,)),
            pltpu.SemaphoreType.DMA((goals * DISTINCT,)),
        ],
        name="pack",
    )(lengths, least, most, *caches, *fresh)


def after(array, *others):
    hbm = pl.BlockSpec(memory_space=pltpu.HBM)
    return pl.pallas_call(
        lambda *refs: None,
        out_shape=jax.ShapeDtypeStruct(array.shape, array.dtype),
        in_specs=[hbm] + [pl.BlockSpec(memory_space=pl.ANY)] * len(others),
        out_specs=hbm,
        input_output_aliases={0: 0},
        compiler_params=pltpu.CompilerParams(vmem_limit_bytes=ROOMY),
        name="after",
    )(array, *others)


def unpack_kernel(slots, arrived, _, result, mark, held, in_sems, out_sems):
    count = result.shape[0]
    share = count // CHUNKS

    def load(p):
        return pltpu.make_async_copy(arrived.at[slots[p]], held.at[p], in_sems.at[p])

    def keep(chunk):
        rows = pl.ds(chunk * share, share)
        return pltpu.make_async_copy(held.at[rows], result.at[rows], out_sems.at[chunk])

    mark[...] = jnp.zeros_like(mark)
    repeat(count, lambda p: load(p).start(), count)
    for chunk in range(CHUNKS):
        repeat(share, lambda p, chunk=chunk: load(p + chunk * share).wait(), share)
        keep(chunk).start()
    for chunk in range(CHUNKS):
        keep(chunk).wait()


def unpack(arrived, slots, other):
    count, (_, suffix, width) = slots.shape[0], arrived.shape
    hbm = pl.BlockSpec(memory_space=pltpu.HBM)
    shape = (count, suffix, width)
    return pl.pallas_call(
        unpack_kernel,
        out_shape=(
            jax.ShapeDtypeStruct(shape, arrived.dtype),
            jax.ShapeDtypeStruct((1, width), jnp.float32),
        ),
        in_specs=[pl.BlockSpec(memory_space=pltpu.SMEM), hbm, pl.BlockSpec(memory_space=pl.ANY)],
        out_specs=(hbm, pl.BlockSpec(memory_space=pltpu.VMEM)),
        scratch_shapes=[
            pltpu.VMEM(shape, arrived.dtype),
            pltpu.SemaphoreType.DMA((count,)),
            pltpu.SemaphoreType.DMA((CHUNKS,)),
        ],
        name="unpack",
    )(slots, arrived, other)


def finish_kernel(counted, step, place, *refs):
    *parts, _, rung_means, next_lengths = refs
    shared = jnp.concatenate([part[...] for part in parts], axis=0)
    peaks, sums, filled = shared[:, 0], shared[:, 1], shared[:, 2]
    top = jnp.max(peaks, axis=0, keepdims=True)
    summed = jnp.sum(sums * jnp.exp(peaks - top), axis=0, keepdims=True)
    rung_means[...] = (top + jnp.log(summed) - jnp.log(counted[...]))[:, :RUNGS]
    order = lax.broadcasted_iota(jnp.int32, filled.shape, 0)
    owner = (order == step[...]).astype(jnp.float32)
    found = lax.dot_general(
        filled, owner, (((0,), (0,)), ((), ())), preferred_element_type=jnp.float32
    )
    order = lax.broadcasted_iota(jnp.int32, found.shape, 0)
    length = jnp.sum(jnp.where(order == place[...], found, 0.0), axis=0, keepdims=True)
    next_lengths[...] = length.astype(jnp.int32) + STEPS


def finish(parts, counted, step, place, other):
    vmem = pl.BlockSpec(memory_space=pltpu.VMEM)
    return pl.pallas_call(
        finish_kernel,
        out_shape=(
            jax.ShapeDtypeStruct((1, RUNGS), jnp.float32),
            jax.ShapeDtypeStruct(step.shape, jnp.int32),
        ),
        in_specs=[vmem] * (3 + len(parts)) + [pl.BlockSpec(memory_space=pl.ANY)],
        out_specs=(vmem, vmem),
        compiler_params=pltpu.CompilerParams(vmem_limit_bytes=ROOMY),
        name="finish",
    )(counted, step, place, *parts, other)


def along(array, axes):
    sides = SIDES
    total = sides[0] * sides[1] * sides[2]
    parts = []
    for steps in itertools.product(*(range(sides[axis]) for axis in axes)):
        pairs = []
        for i in range(total):
            goal = [i // (sides[1] * sides[2]), i // sides[2] % sides[1], i % sides[2]]
            for axis, step in zip(axes, steps):
                goal[axis] = (goal[axis] + step) % sides[axis]
            pairs.append((i, (goal[0] * sides[1] + goal[1]) * sides[2] + goal[2]))
        parts.append(lax.ppermute(array, "particle", pairs) if any(steps) else array)
    return parts


def devices():
    tall, wide, cores = SIDES
    return [
        (i, z, i % cores + cores * (z % 2)) for i in range(tall * wide * cores) for z in range(PLANES)
    ]


def columns_of(array):
    tall, wide, cores = SIDES
    parts = []
    for step in range(tall):
        pairs = []
        for i, z, copy in devices():
            y, x = i // (wide * cores), i // cores % wide
            goal = (((y + step) % tall) * wide + (x + copy) % wide) * cores + i % cores
            pairs.append((i * PLANES + z, goal * PLANES + z))
        parts.append(lax.ppermute(array, ("particle", "tensor"), pairs))
    return parts


def copies_of(array):
    parts = []
    for other in range(1, 4):
        pairs = [
            (i * PLANES + z, (i ^ other % 2) * PLANES + (z ^ other // 2)) for i, z, _ in devices()
        ]
        parts.append(lax.ppermute(array, ("particle", "tensor"), pairs))
    return parts


def shards(
    queries,
    new_keys,
    new_values,
    key_cache,
    value_cache,
    prompt_keys,
    prompt_values,
    lengths,
    prior,
    reward_dir,
    rungs,
    ancestors,
):
    per_device = queries.shape[0]
    suffix = key_cache.shape[1]
    groups = HEADS // KV_HEADS
    scale = HEAD_DIM ** (-0.5)
    sources = lax.axis_size("particle")
    device = lax.axis_index("particle")

    low = -jnp.inf
    shard = jnp.maximum(
        jnp.pad(prompt_keys, ((0, 0), (0, HEAD_DIM)), constant_values=low),
        jnp.pad(prompt_values, ((0, 0), (HEAD_DIM, 0)), constant_values=low),
    )
    column = shard
    for bit in (1, 2):
        swapped = lax.ppermute(column, "particle", [(i, i ^ bit * 8) for i in range(sources)])
        column = jnp.concatenate([column, swapped], axis=0)
    plane = jnp.concatenate(along(column, (1,)), axis=0)
    prompt = jnp.concatenate(along(plane, (2,)), axis=0)
    all_keys = prompt[:, :HEAD_DIM]
    all_values = prompt[:, HEAD_DIM:]

    wanted = ancestors.reshape(sources, per_device)
    owner = wanted // per_device
    local = wanted % per_device
    chosen = owner == device
    least = jnp.min(jnp.where(chosen, local, per_device - 1), axis=1)
    most = jnp.max(jnp.where(chosen, local, 0), axis=1)
    mine = lax.dynamic_slice_in_dim(ancestors, device * per_device, per_device)
    mine_owner = mine // per_device
    same_owner = mine_owner[:, None] == mine_owner[None, :]
    first = jnp.min(jnp.where(same_owner, mine[None, :], sources * per_device), axis=1)
    slot = mine_owner * DISTINCT + (mine != first).astype(jnp.int32)

    exchange = functools.partial(
        lax.all_to_all, axis_name="particle", split_axis=0, concat_axis=0, tiled=True
    )
    places = (lengths, least, most)
    (outgoing_keys,) = pack((key_cache,), (new_keys,), *places, False)
    arrived_keys = exchange(after(outgoing_keys, column))
    outgoing_values, written_keys, written_values = pack(
        (key_cache, value_cache), (new_keys, new_values), *places, True
    )
    arrived_values = exchange(after(outgoing_values, arrived_keys))
    next_keys, mark = unpack(arrived_keys, slot, column)

    query = queries.reshape(per_device, STEPS, groups, HEAD_DIM)
    front = (
        jnp.einsum("pshd,nd->pshn", query, all_keys, preferred_element_type=jnp.float32) * scale
    )
    back = (
        jnp.einsum("pshd,pld->pshl", query, written_keys, preferred_element_type=jnp.float32)
        * scale
    )
    position = jnp.arange(suffix, dtype=jnp.int32)
    later = jnp.arange(STEPS, dtype=jnp.int32)
    visible = position[None, None, :] < lengths[:, None, None] + 1 + later[None, :, None]
    back = jnp.where(visible[:, :, None, :], back, -jnp.inf)
    peak = jnp.maximum(jnp.max(front, axis=-1), jnp.max(back, axis=-1))
    front = jnp.exp(front - peak[..., None])
    back = jnp.exp(back - peak[..., None])
    total = jnp.sum(front, axis=-1) + jnp.sum(back, axis=-1)
    mixed = jnp.einsum(
        "pshn,nd->pshd",
        front.astype(jnp.bfloat16),
        all_values,
        preferred_element_type=jnp.float32,
    ) + jnp.einsum(
        "pshl,pld->pshd",
        back.astype(jnp.bfloat16),
        written_values,
        preferred_element_type=jnp.float32,
    )
    output = (mixed / total[..., None]).reshape(per_device, STEPS, -1)
    attention = output.astype(jnp.bfloat16)

    partial_reward = jnp.sum(output * reward_dir[None, None, :], axis=(1, 2))
    weights = prior + lax.psum(partial_reward, "tensor")
    own_rungs = lax.dynamic_slice_in_dim(rungs, device * per_device, per_device)
    ladder = jnp.arange(RUNGS, dtype=jnp.int32)
    member = own_rungs[:, None] == ladder[None, :]
    local_peak = jnp.max(jnp.where(member, weights[:, None], -1e30), axis=0)
    local_sum = jnp.sum(
        jnp.where(member, jnp.exp(weights[:, None] - local_peak[None, :]), 0.0), axis=0
    )
    spare = per_device - RUNGS
    shared = jnp.stack(
        [
            jnp.pad(local_peak, (0, spare)),
            jnp.pad(local_sum, (0, spare), constant_values=1.0),
            lengths.astype(jnp.float32) + mark[0, :per_device],
        ]
    )[None]
    near = jnp.concatenate(along(shared, (2,)), axis=0)
    cross = jnp.concatenate(columns_of(near), axis=0)
    next_values, mark = unpack(arrived_values, slot, near)
    parts = [cross] + copies_of(cross)

    counted = jnp.sum((rungs[:, None] == ladder[None, :]).astype(jnp.float32), axis=0)
    tall, wide, cores = SIDES
    up = (device // (wide * cores) - mine_owner // (wide * cores)) % tall
    right = (device // cores % wide - mine_owner // cores % wide) % wide
    across = (device % cores - mine_owner % cores) % cores
    copy = device % cores + cores * (lax.axis_index("tensor") % 2)
    part = right ^ copy
    step = (part * tall + up) * cores + (across ^ part % cores)
    rung_means, next_lengths = finish(
        parts,
        jnp.pad(counted, (0, spare), constant_values=1.0)[None],
        step[None],
        (mine % per_device)[None],
        mark,
    )
    rung_means = rung_means[0]
    next_lengths = next_lengths[0]
    return (attention, weights, rung_means, next_keys, next_values, next_lengths)


def solution(mesh):
    placed = (
        P("particle", None, "tensor"),
        P("particle", None, "tensor"),
        P("particle", None, "tensor"),
        P("particle", None, "tensor"),
        P("particle", None, "tensor"),
        P("particle", "tensor"),
        P("particle", "tensor"),
        P("particle"),
        P("particle"),
        P("tensor"),
        P(),
        P(),
    )
    return jax.shard_map(
        shards,
        mesh=mesh,
        in_specs=placed,
        out_specs=(
            P("particle", None, "tensor"),
            P("particle"),
            P(),
            P("particle", None, "tensor"),
            P("particle", None, "tensor"),
            P("particle"),
        ),
        check_vma=False,
    )
```

```python
import functools
import itertools

import jax
import jax.numpy as jnp
from jax import lax
from jax.experimental import pallas as pl
from jax.experimental.pallas import tpu as pltpu
from jax.sharding import PartitionSpec as P

HEADS = 64
KV_HEADS = 8
HEAD_DIM = 128
STEPS = 2
RUNGS = 8
DISTINCT = 2
SIDES = (4, 4, 2)
PLANES = 8
WINDOW = 32
CHUNKS = 4
GROUP = 2
ROOMY = 58 << 20


def pack_kernel(sends, lengths, least, most, *refs):
    caches, fresh, outs = refs[:2], refs[2:4], refs[4:-3]
    held, in_sems, out_sems = refs[-3:]
    count, suffix, _ = caches[0].shape
    goals = least.shape[0]
    share = count // CHUNKS

    def load(chunk, n):
        rows = pl.ds(chunk * share, share)
        return pltpu.make_async_copy(
            caches[n].at[rows], held.at[rows, pl.ds(n * suffix, suffix)], in_sems.at[chunk * 2 + n]
        )

    def keep(n):
        return pltpu.make_async_copy(
            held.at[:, pl.ds(n * suffix, suffix)], outs[n], out_sems.at[n]
        )

    def low(d):
        return pltpu.make_async_copy(held.at[least[d]], outs[0].at[2 * d], out_sems.at[2 * d])

    def high(d):
        return pltpu.make_async_copy(
            held.at[most[d]], outs[0].at[2 * d + 1], out_sems.at[2 * d + 1]
        )

    def patch(group):
        found = []
        for i in range(GROUP):
            p = group * GROUP + i
            length = lengths[p]
            base = pl.multiple_of(jnp.minimum(length // 16 * 16, suffix - WINDOW), 16)
            for n in range(2):
                place = (p, pl.ds(base + n * suffix, WINDOW))
                block = held[place].astype(jnp.float32)
                lines = fresh[n][p].astype(jnp.float32)
                row = lax.broadcasted_iota(jnp.int32, block.shape, 0) + base
                for offset in range(STEPS):
                    block = jnp.where(row == length + offset, lines[offset : offset + 1], block)
                found.append((place, block.astype(held.dtype)))
        for place, block in found:
            held[place] = block

    for chunk in range(CHUNKS):
        for n in range(2):
            load(chunk, n).start()
    for chunk in range(CHUNKS):
        for n in range(2):
            load(chunk, n).wait()
        groups = share // GROUP
        repeat(groups, lambda g, chunk=chunk: patch(g + chunk * groups), 1)
    if sends:
        repeat(goals, lambda d: (low(d).start(), high(d).start()), 8)
        repeat(goals, lambda d: (low(d).wait(), high(d).wait()), 8)
    else:
        for n in range(2):
            keep(n).start()
        for n in range(2):
            keep(n).wait()


def repeat(count, body, unroll=4):
    def step(i, carry):
        body(i)
        return carry

    lax.fori_loop(0, count, step, 0, unroll=unroll)


def pack(caches, fresh, lengths, least, most, sends):
    cache = caches[0]
    (count, suffix, width), goals = cache.shape, least.shape[0]
    smem = pl.BlockSpec(memory_space=pltpu.SMEM)
    hbm = pl.BlockSpec(memory_space=pltpu.HBM)
    vmem = pl.BlockSpec(memory_space=pltpu.VMEM)
    if sends:
        shapes = [(goals * DISTINCT, 2 * suffix, width)]
    else:
        shapes = [cache.shape] * 2
    return pl.pallas_call(
        functools.partial(pack_kernel, sends),
        out_shape=[jax.ShapeDtypeStruct(shape, cache.dtype) for shape in shapes],
        in_specs=[smem] * 3 + [hbm] * 2 + [vmem] * 2,
        out_specs=[hbm] * len(shapes),
        scratch_shapes=[
            pltpu.VMEM((count, 2 * suffix, width), cache.dtype),
            pltpu.SemaphoreType.DMA((2 * CHUNKS,)),
            pltpu.SemaphoreType.DMA((goals * DISTINCT,)),
        ],
        name="pack",
    )(lengths, least, most, *caches, *fresh)


def after(array, *others):
    hbm = pl.BlockSpec(memory_space=pltpu.HBM)
    return pl.pallas_call(
        lambda *refs: None,
        out_shape=jax.ShapeDtypeStruct(array.shape, array.dtype),
        in_specs=[hbm] + [pl.BlockSpec(memory_space=pl.ANY)] * len(others),
        out_specs=hbm,
        input_output_aliases={0: 0},
        compiler_params=pltpu.CompilerParams(vmem_limit_bytes=ROOMY),
        name="after",
    )(array, *others)


def unpack_kernel(slots, arrived, _, next_keys, next_values, mark, held, in_sems, out_sems):
    count, suffix, _ = next_keys.shape
    share = count // CHUNKS

    def load(p):
        return pltpu.make_async_copy(arrived.at[slots[p]], held.at[p], in_sems.at[p])

    def keep(chunk, half):
        rows = pl.ds(chunk * share, share)
        return pltpu.make_async_copy(
            held.at[rows, pl.ds(half * suffix, suffix)],
            (next_keys, next_values)[half].at[rows],
            out_sems.at[chunk * 2 + half],
        )

    mark[...] = jnp.zeros_like(mark)
    repeat(count, lambda p: load(p).start(), count)
    for chunk in range(CHUNKS):
        repeat(share, lambda p, chunk=chunk: load(p + chunk * share).wait(), share)
        for half in range(2):
            keep(chunk, half).start()
    for chunk in range(CHUNKS):
        for half in range(2):
            keep(chunk, half).wait()


def unpack(arrived, slots, other):
    count, (_, length, width) = slots.shape[0], arrived.shape
    hbm = pl.BlockSpec(memory_space=pltpu.HBM)
    shape = jax.ShapeDtypeStruct((count, length // 2, width), arrived.dtype)
    return pl.pallas_call(
        unpack_kernel,
        out_shape=(shape, shape, jax.ShapeDtypeStruct((1, width), jnp.float32)),
        in_specs=[pl.BlockSpec(memory_space=pltpu.SMEM), hbm, pl.BlockSpec(memory_space=pl.ANY)],
        out_specs=(hbm, hbm, pl.BlockSpec(memory_space=pltpu.VMEM)),
        scratch_shapes=[
            pltpu.VMEM((count, length, width), arrived.dtype),
            pltpu.SemaphoreType.DMA((count,)),
            pltpu.SemaphoreType.DMA((2 * CHUNKS,)),
        ],
        name="unpack",
    )(slots, arrived, other)


def finish_kernel(counted, step, place, *refs):
    *parts, _, rung_means, next_lengths = refs
    shared = jnp.concatenate([part[...] for part in parts], axis=0)
    peaks, sums, filled = shared[:, 0], shared[:, 1], shared[:, 2]
    top = jnp.max(peaks, axis=0, keepdims=True)
    summed = jnp.sum(sums * jnp.exp(peaks - top), axis=0, keepdims=True)
    rung_means[...] = (top + jnp.log(summed) - jnp.log(counted[...]))[:, :RUNGS]
    order = lax.broadcasted_iota(jnp.int32, filled.shape, 0)
    owner = (order == step[...]).astype(jnp.float32)
    found = lax.dot_general(
        filled, owner, (((0,), (0,)), ((), ())), preferred_element_type=jnp.float32
    )
    order = lax.broadcasted_iota(jnp.int32, found.shape, 0)
    length = jnp.sum(jnp.where(order == place[...], found, 0.0), axis=0, keepdims=True)
    next_lengths[...] = length.astype(jnp.int32) + STEPS


def finish(parts, counted, step, place, other):
    vmem = pl.BlockSpec(memory_space=pltpu.VMEM)
    return pl.pallas_call(
        finish_kernel,
        out_shape=(
            jax.ShapeDtypeStruct((1, RUNGS), jnp.float32),
            jax.ShapeDtypeStruct(step.shape, jnp.int32),
        ),
        in_specs=[vmem] * (3 + len(parts)) + [pl.BlockSpec(memory_space=pl.ANY)],
        out_specs=(vmem, vmem),
        compiler_params=pltpu.CompilerParams(vmem_limit_bytes=ROOMY),
        name="finish",
    )(counted, step, place, *parts, other)


def along(array, axes):
    sides = SIDES
    total = sides[0] * sides[1] * sides[2]
    parts = []
    for steps in itertools.product(*(range(sides[axis]) for axis in axes)):
        pairs = []
        for i in range(total):
            goal = [i // (sides[1] * sides[2]), i // sides[2] % sides[1], i % sides[2]]
            for axis, step in zip(axes, steps):
                goal[axis] = (goal[axis] + step) % sides[axis]
            pairs.append((i, (goal[0] * sides[1] + goal[1]) * sides[2] + goal[2]))
        parts.append(lax.ppermute(array, "particle", pairs) if any(steps) else array)
    return parts


def devices():
    tall, wide, cores = SIDES
    return [
        (i, z, i % cores + cores * (z % 2)) for i in range(tall * wide * cores) for z in range(PLANES)
    ]


def columns_of(array):
    tall, wide, cores = SIDES
    parts = []
    for step in range(tall):
        pairs = []
        for i, z, copy in devices():
            y, x = i // (wide * cores), i // cores % wide
            goal = (((y + step) % tall) * wide + (x + copy) % wide) * cores + i % cores
            pairs.append((i * PLANES + z, goal * PLANES + z))
        parts.append(lax.ppermute(array, ("particle", "tensor"), pairs))
    return parts


def copies_of(array):
    parts = []
    for other in range(1, 4):
        pairs = [
            (i * PLANES + z, (i ^ other % 2) * PLANES + (z ^ other // 2)) for i, z, _ in devices()
        ]
        parts.append(lax.ppermute(array, ("particle", "tensor"), pairs))
    return parts


def shards(
    queries,
    new_keys,
    new_values,
    key_cache,
    value_cache,
    prompt_keys,
    prompt_values,
    lengths,
    prior,
    reward_dir,
    rungs,
    ancestors,
):
    per_device = queries.shape[0]
    suffix = key_cache.shape[1]
    groups = HEADS // KV_HEADS
    scale = HEAD_DIM ** (-0.5)
    sources = lax.axis_size("particle")
    device = lax.axis_index("particle")

    wanted = ancestors.reshape(sources, per_device)
    owner = wanted // per_device
    local = wanted % per_device
    chosen = owner == device
    least = jnp.min(jnp.where(chosen, local, per_device - 1), axis=1)
    most = jnp.max(jnp.where(chosen, local, 0), axis=1)
    mine = lax.dynamic_slice_in_dim(ancestors, device * per_device, per_device)
    mine_owner = mine // per_device
    same_owner = mine_owner[:, None] == mine_owner[None, :]
    first = jnp.min(jnp.where(same_owner, mine[None, :], sources * per_device), axis=1)
    slot = mine_owner * DISTINCT + (mine != first).astype(jnp.int32)

    low = -jnp.inf
    shard = jnp.maximum(
        jnp.pad(prompt_keys, ((0, 0), (0, HEAD_DIM)), constant_values=low),
        jnp.pad(prompt_values, ((0, 0), (HEAD_DIM, 0)), constant_values=low),
    )
    column = shard
    for bit in (1, 2):
        swapped = lax.ppermute(column, "particle", [(i, i ^ bit * 8) for i in range(sources)])
        column = jnp.concatenate([column, swapped], axis=0)
        if bit == 1:
            column = column + jnp.minimum(least[0], 0).astype(column.dtype)
    columns = along(column, (1,))
    prompt = jnp.concatenate(along(jnp.concatenate(columns, axis=0), (2,)), axis=0)
    all_keys = prompt[:, :HEAD_DIM]
    all_values = prompt[:, HEAD_DIM:]

    given = ((key_cache, value_cache), (new_keys, new_values), lengths, least, most)
    (outgoing,) = pack(*given, True)
    arrived = lax.all_to_all(
        after(outgoing, *columns[1:]), "particle", split_axis=0, concat_axis=0, tiled=True
    )
    written_keys, written_values = pack(*given, False)

    query = queries.reshape(per_device, STEPS, groups, HEAD_DIM)
    front = (
        jnp.einsum("pshd,nd->pshn", query, all_keys, preferred_element_type=jnp.float32) * scale
    )
    back = (
        jnp.einsum("pshd,pld->pshl", query, written_keys, preferred_element_type=jnp.float32)
        * scale
    )
    position = jnp.arange(suffix, dtype=jnp.int32)
    later = jnp.arange(STEPS, dtype=jnp.int32)
    visible = position[None, None, :] < lengths[:, None, None] + 1 + later[None, :, None]
    back = jnp.where(visible[:, :, None, :], back, -jnp.inf)
    peak = jnp.maximum(jnp.max(front, axis=-1), jnp.max(back, axis=-1))
    front = jnp.exp(front - peak[..., None])
    back = jnp.exp(back - peak[..., None])
    total = jnp.sum(front, axis=-1) + jnp.sum(back, axis=-1)
    mixed = jnp.einsum(
        "pshn,nd->pshd",
        front.astype(jnp.bfloat16),
        all_values,
        preferred_element_type=jnp.float32,
    ) + jnp.einsum(
        "pshl,pld->pshd",
        back.astype(jnp.bfloat16),
        written_values,
        preferred_element_type=jnp.float32,
    )
    output = (mixed / total[..., None]).reshape(per_device, STEPS, -1)
    attention = output.astype(jnp.bfloat16)

    partial_reward = jnp.sum(output * reward_dir[None, None, :], axis=(1, 2))
    weights = prior + lax.psum(partial_reward, "tensor")
    own_rungs = lax.dynamic_slice_in_dim(rungs, device * per_device, per_device)
    ladder = jnp.arange(RUNGS, dtype=jnp.int32)
    member = own_rungs[:, None] == ladder[None, :]
    local_peak = jnp.max(jnp.where(member, weights[:, None], -1e30), axis=0)
    local_sum = jnp.sum(
        jnp.where(member, jnp.exp(weights[:, None] - local_peak[None, :]), 0.0), axis=0
    )
    spare = per_device - RUNGS
    shared = jnp.stack(
        [
            jnp.pad(local_peak, (0, spare)),
            jnp.pad(local_sum, (0, spare), constant_values=1.0),
            lengths.astype(jnp.float32),
        ]
    )[None]
    near = jnp.concatenate(along(shared, (2,)), axis=0)
    near = after(near, attention)
    cross = jnp.concatenate(columns_of(near), axis=0)
    next_keys, next_values, mark = unpack(arrived, slot, near)
    parts = [cross] + copies_of(cross)

    counted = jnp.sum((rungs[:, None] == ladder[None, :]).astype(jnp.float32), axis=0)
    tall, wide, cores = SIDES
    up = (device // (wide * cores) - mine_owner // (wide * cores)) % tall
    right = (device // cores % wide - mine_owner // cores % wide) % wide
    across = (device % cores - mine_owner % cores) % cores
    copy = device % cores + cores * (lax.axis_index("tensor") % 2)
    part = right ^ copy
    step = (part * tall + up) * cores + (across ^ part % cores)
    rung_means, next_lengths = finish(
        parts,
        jnp.pad(counted, (0, spare), constant_values=1.0)[None],
        step[None],
        (mine % per_device)[None],
        mark,
    )
    rung_means = rung_means[0]
    next_lengths = next_lengths[0]
    return (attention, weights, rung_means, next_keys, next_values, next_lengths)


def solution(mesh):
    placed = (
        P("particle", None, "tensor"),
        P("particle", None, "tensor"),
        P("particle", None, "tensor"),
        P("particle", None, "tensor"),
        P("particle", None, "tensor"),
        P("particle", "tensor"),
        P("particle", "tensor"),
        P("particle"),
        P("particle"),
        P("tensor"),
        P(),
        P(),
    )
    return jax.shard_map(
        shards,
        mesh=mesh,
        in_specs=placed,
        out_specs=(
            P("particle", None, "tensor"),
            P("particle"),
            P(),
            P("particle", None, "tensor"),
            P("particle", None, "tensor"),
            P("particle"),
        ),
        check_vma=False,
    )
```

```python
import functools
import itertools

import jax
import jax.numpy as jnp
from jax import lax
from jax.experimental import pallas as pl
from jax.experimental.pallas import tpu as pltpu
from jax.sharding import PartitionSpec as P

HEADS = 64
KV_HEADS = 8
HEAD_DIM = 128
STEPS = 2
RUNGS = 8
DISTINCT = 2
SIDES = (4, 4, 2)
PLANES = 8
WINDOW = 32
CHUNKS = 4
GROUP = 2
ROOMY = 58 << 20


def pack_kernel(keeps, lengths, least, most, *refs):
    number = (len(refs) - 5) // (2 + keeps)
    caches, fresh, (packed, *written) = refs[:number], refs[number : 2 * number], refs[2 * number : -4]
    held, in_sems, out_sems, send_sems = refs[-4:]
    count, suffix, _ = caches[0].shape
    goals = least.shape[0]
    share = count // CHUNKS

    def load(chunk, n):
        rows = pl.ds(chunk * share, share)
        return pltpu.make_async_copy(
            caches[n].at[rows], held.at[n, rows], in_sems.at[chunk * number + n]
        )

    def keep(n):
        return pltpu.make_async_copy(held.at[n], written[n], out_sems.at[n])

    def low(d):
        return pltpu.make_async_copy(
            held.at[number - 1, least[d]], packed.at[2 * d], send_sems.at[2 * d]
        )

    def high(d):
        return pltpu.make_async_copy(
            held.at[number - 1, most[d]], packed.at[2 * d + 1], send_sems.at[2 * d + 1]
        )

    def patch(group):
        found = []
        for i in range(GROUP):
            p = group * GROUP + i
            length = lengths[p]
            base = pl.multiple_of(jnp.minimum(length // 16 * 16, suffix - WINDOW), 16)
            for n in range(number):
                place = (n, p, pl.ds(base, WINDOW))
                block = held[place].astype(jnp.float32)
                lines = fresh[n][p].astype(jnp.float32)
                row = lax.broadcasted_iota(jnp.int32, block.shape, 0) + base
                for offset in range(STEPS):
                    block = jnp.where(row == length + offset, lines[offset : offset + 1], block)
                found.append((place, block.astype(held.dtype)))
        for place, block in found:
            held[place] = block

    for chunk in range(CHUNKS):
        for n in range(number):
            load(chunk, n).start()
    for chunk in range(CHUNKS):
        for n in range(number):
            load(chunk, n).wait()
        groups = share // GROUP
        repeat(groups, lambda g, chunk=chunk: patch(g + chunk * groups), 1)
    repeat(goals, lambda d: (low(d).start(), high(d).start()))
    for n in range(number * keeps):
        keep(n).start()
    repeat(goals, lambda d: (low(d).wait(), high(d).wait()))
    for n in range(number * keeps):
        keep(n).wait()


def repeat(count, body, unroll=4):
    def step(i, carry):
        body(i)
        return carry

    lax.fori_loop(0, count, step, 0, unroll=unroll)


def pack(caches, fresh, lengths, least, most, keeps):
    cache, number = caches[0], len(caches)
    count, goals = cache.shape[0], least.shape[0]
    smem = pl.BlockSpec(memory_space=pltpu.SMEM)
    hbm = pl.BlockSpec(memory_space=pltpu.HBM)
    vmem = pl.BlockSpec(memory_space=pltpu.VMEM)
    return pl.pallas_call(
        functools.partial(pack_kernel, keeps),
        out_shape=[jax.ShapeDtypeStruct((goals * DISTINCT,) + cache.shape[1:], cache.dtype)]
        + [jax.ShapeDtypeStruct(cache.shape, cache.dtype)] * (number * keeps),
        in_specs=[smem] * 3 + [hbm] * number + [vmem] * number,
        out_specs=[hbm] * (1 + number * keeps),
        scratch_shapes=[
            pltpu.VMEM((number,) + cache.shape, cache.dtype),
            pltpu.SemaphoreType.DMA((number * CHUNKS,)),
            pltpu.SemaphoreType.DMA((number,)),
            pltpu.SemaphoreType.DMA((goals * DISTINCT,)),
        ],
        name="pack",
    )(lengths, least, most, *caches, *fresh)


def after(array, *others):
    hbm = pl.BlockSpec(memory_space=pltpu.HBM)
    return pl.pallas_call(
        lambda *refs: None,
        out_shape=jax.ShapeDtypeStruct(array.shape, array.dtype),
        in_specs=[hbm] + [pl.BlockSpec(memory_space=pl.ANY)] * len(others),
        out_specs=hbm,
        input_output_aliases={0: 0},
        compiler_params=pltpu.CompilerParams(vmem_limit_bytes=ROOMY),
        name="after",
    )(array, *others)


def unpack_kernel(slots, arrived, _, result, mark, held, in_sems, out_sems):
    count = result.shape[0]
    share = count // CHUNKS

    def load(p):
        return pltpu.make_async_copy(arrived.at[slots[p]], held.at[p], in_sems.at[p])

    def keep(chunk):
        rows = pl.ds(chunk * share, share)
        return pltpu.make_async_copy(held.at[rows], result.at[rows], out_sems.at[chunk])

    mark[...] = jnp.zeros_like(mark)
    repeat(count, lambda p: load(p).start(), count)
    for chunk in range(CHUNKS):
        repeat(share, lambda p, chunk=chunk: load(p + chunk * share).wait(), share)
        keep(chunk).start()
    for chunk in range(CHUNKS):
        keep(chunk).wait()


def unpack(arrived, slots, other):
    count, (_, suffix, width) = slots.shape[0], arrived.shape
    hbm = pl.BlockSpec(memory_space=pltpu.HBM)
    shape = (count, suffix, width)
    return pl.pallas_call(
        unpack_kernel,
        out_shape=(
            jax.ShapeDtypeStruct(shape, arrived.dtype),
            jax.ShapeDtypeStruct((1, width), jnp.float32),
        ),
        in_specs=[pl.BlockSpec(memory_space=pltpu.SMEM), hbm, pl.BlockSpec(memory_space=pl.ANY)],
        out_specs=(hbm, pl.BlockSpec(memory_space=pltpu.VMEM)),
        scratch_shapes=[
            pltpu.VMEM(shape, arrived.dtype),
            pltpu.SemaphoreType.DMA((count,)),
            pltpu.SemaphoreType.DMA((CHUNKS,)),
        ],
        name="unpack",
    )(slots, arrived, other)


def finish_kernel(counted, step, place, *refs):
    *parts, _, rung_means, next_lengths = refs
    shared = jnp.concatenate([part[...] for part in parts], axis=0)
    peaks, sums, filled = shared[:, 0], shared[:, 1], shared[:, 2]
    top = jnp.max(peaks, axis=0, keepdims=True)
    summed = jnp.sum(sums * jnp.exp(peaks - top), axis=0, keepdims=True)
    rung_means[...] = (top + jnp.log(summed) - jnp.log(counted[...]))[:, :RUNGS]
    order = lax.broadcasted_iota(jnp.int32, filled.shape, 0)
    owner = (order == step[...]).astype(jnp.float32)
    found = lax.dot_general(
        filled, owner, (((0,), (0,)), ((), ())), preferred_element_type=jnp.float32
    )
    order = lax.broadcasted_iota(jnp.int32, found.shape, 0)
    length = jnp.sum(jnp.where(order == place[...], found, 0.0), axis=0, keepdims=True)
    next_lengths[...] = length.astype(jnp.int32) + STEPS


def finish(parts, counted, step, place, other):
    vmem = pl.BlockSpec(memory_space=pltpu.VMEM)
    return pl.pallas_call(
        finish_kernel,
        out_shape=(
            jax.ShapeDtypeStruct((1, RUNGS), jnp.float32),
            jax.ShapeDtypeStruct(step.shape, jnp.int32),
        ),
        in_specs=[vmem] * (3 + len(parts)) + [pl.BlockSpec(memory_space=pl.ANY)],
        out_specs=(vmem, vmem),
        compiler_params=pltpu.CompilerParams(vmem_limit_bytes=ROOMY),
        name="finish",
    )(counted, step, place, *parts, other)


def along(array, axes):
    sides = SIDES
    total = sides[0] * sides[1] * sides[2]
    parts = []
    for steps in itertools.product(*(range(sides[axis]) for axis in axes)):
        pairs = []
        for i in range(total):
            goal = [i // (sides[1] * sides[2]), i // sides[2] % sides[1], i % sides[2]]
            for axis, step in zip(axes, steps):
                goal[axis] = (goal[axis] + step) % sides[axis]
            pairs.append((i, (goal[0] * sides[1] + goal[1]) * sides[2] + goal[2]))
        parts.append(lax.ppermute(array, "particle", pairs) if any(steps) else array)
    return parts


def half_of(array):
    tall, wide, cores = SIDES
    parts = []
    for hop, step in itertools.product(range(2), range(2)):
        pairs = []
        for i in range(tall * wide * cores):
            y, x, core = i // (wide * cores), i // cores % wide, i % cores
            goal = (y ^ 2 * hop) * wide + (x + 2 * core + step) % wide
            pairs.append((i, goal * cores + core))
        parts.append(lax.ppermute(array, "particle", pairs))
    return parts


def devices():
    tall, wide, cores = SIDES
    return [
        (i, z, i % cores + cores * (z % 2)) for i in range(tall * wide * cores) for z in range(PLANES)
    ]


def columns_of(array):
    tall, wide, cores = SIDES
    parts = []
    for step in range(tall):
        pairs = []
        for i, z, copy in devices():
            y, x = i // (wide * cores), i // cores % wide
            goal = (((y + step) % tall) * wide + (x + copy) % wide) * cores + i % cores
            pairs.append((i * PLANES + z, goal * PLANES + z))
        parts.append(lax.ppermute(array, ("particle", "tensor"), pairs))
    return parts


def copies_of(array):
    parts = []
    for other in range(1, 4):
        pairs = [
            (i * PLANES + z, (i ^ other % 2) * PLANES + (z ^ other // 2)) for i, z, _ in devices()
        ]
        parts.append(lax.ppermute(array, ("particle", "tensor"), pairs))
    return parts


def shards(
    queries,
    new_keys,
    new_values,
    key_cache,
    value_cache,
    prompt_keys,
    prompt_values,
    lengths,
    prior,
    reward_dir,
    rungs,
    ancestors,
):
    per_device = queries.shape[0]
    suffix = key_cache.shape[1]
    groups = HEADS // KV_HEADS
    scale = HEAD_DIM ** (-0.5)
    sources = lax.axis_size("particle")
    device = lax.axis_index("particle")

    wanted = ancestors.reshape(sources, per_device)
    owner = wanted // per_device
    local = wanted % per_device
    chosen = owner == device
    least = jnp.min(jnp.where(chosen, local, per_device - 1), axis=1)
    most = jnp.max(jnp.where(chosen, local, 0), axis=1)
    mine = lax.dynamic_slice_in_dim(ancestors, device * per_device, per_device)
    mine_owner = mine // per_device
    same_owner = mine_owner[:, None] == mine_owner[None, :]
    first = jnp.min(jnp.where(same_owner, mine[None, :], sources * per_device), axis=1)
    slot = mine_owner * DISTINCT + (mine != first).astype(jnp.int32)

    low = -jnp.inf
    shard = jnp.maximum(
        jnp.pad(prompt_keys, ((0, 0), (0, HEAD_DIM)), constant_values=low),
        jnp.pad(prompt_values, ((0, 0), (HEAD_DIM, 0)), constant_values=low),
    )
    chip = jnp.concatenate(along(shard, (2,)), axis=0)
    chip = chip + jnp.minimum(least[0], 0).astype(chip.dtype)
    beside = lax.ppermute(chip, "particle", [(i, i ^ 8) for i in range(sources)])
    column = jnp.concatenate([chip, beside], axis=0)
    half = jnp.concatenate(half_of(column), axis=0)
    prompt = jnp.concatenate(along(half, (2,)), axis=0)
    all_keys = prompt[:, :HEAD_DIM]
    all_values = prompt[:, HEAD_DIM:]

    exchange = functools.partial(
        lax.all_to_all, axis_name="particle", split_axis=0, concat_axis=0, tiled=True
    )
    places = (lengths, least, most)
    (outgoing_keys,) = pack((key_cache,), (new_keys,), *places, False)
    arrived_keys = exchange(after(outgoing_keys, column))
    outgoing_values, written_keys, written_values = pack(
        (key_cache, value_cache), (new_keys, new_values), *places, True
    )
    arrived_values = exchange(after(outgoing_values, arrived_keys))
    next_keys, mark = unpack(arrived_keys, slot, column)

    query = queries.reshape(per_device, STEPS, groups, HEAD_DIM)
    front = (
        jnp.einsum("pshd,nd->pshn", query, all_keys, preferred_element_type=jnp.float32) * scale
    )
    back = (
        jnp.einsum("pshd,pld->pshl", query, written_keys, preferred_element_type=jnp.float32)
        * scale
    )
    position = jnp.arange(suffix, dtype=jnp.int32)
    later = jnp.arange(STEPS, dtype=jnp.int32)
    visible = position[None, None, :] < lengths[:, None, None] + 1 + later[None, :, None]
    back = jnp.where(visible[:, :, None, :], back, -jnp.inf)
    peak = jnp.maximum(jnp.max(front, axis=-1), jnp.max(back, axis=-1))
    front = jnp.exp(front - peak[..., None])
    back = jnp.exp(back - peak[..., None])
    total = jnp.sum(front, axis=-1) + jnp.sum(back, axis=-1)
    mixed = jnp.einsum(
        "pshn,nd->pshd",
        front.astype(jnp.bfloat16),
        all_values,
        preferred_element_type=jnp.float32,
    ) + jnp.einsum(
        "pshl,pld->pshd",
        back.astype(jnp.bfloat16),
        written_values,
        preferred_element_type=jnp.float32,
    )
    output = (mixed / total[..., None]).reshape(per_device, STEPS, -1)
    attention = output.astype(jnp.bfloat16)

    partial_reward = jnp.sum(output * reward_dir[None, None, :], axis=(1, 2))
    reward = partial_reward
    for bit in (1, 2, 4):
        pairs = [(i, i ^ bit) for i in range(PLANES)]
        reward = reward + lax.ppermute(reward, "tensor", pairs)
    weights = prior + reward
    own_rungs = lax.dynamic_slice_in_dim(rungs, device * per_device, per_device)
    ladder = jnp.arange(RUNGS, dtype=jnp.int32)
    member = own_rungs[:, None] == ladder[None, :]
    local_peak = jnp.max(jnp.where(member, weights[:, None], -1e30), axis=0)
    local_sum = jnp.sum(
        jnp.where(member, jnp.exp(weights[:, None] - local_peak[None, :]), 0.0), axis=0
    )
    spare = per_device - RUNGS
    shared = jnp.stack(
        [
            jnp.pad(local_peak, (0, spare)),
            jnp.pad(local_sum, (0, spare), constant_values=1.0),
            lengths.astype(jnp.float32),
        ]
    )[None]
    near = jnp.concatenate(along(shared, (2,)), axis=0)
    near = after(near, attention, mark)
    cross = jnp.concatenate(columns_of(near), axis=0)
    next_values, mark = unpack(arrived_values, slot, near)
    parts = [cross] + copies_of(cross)

    counted = jnp.sum((rungs[:, None] == ladder[None, :]).astype(jnp.float32), axis=0)
    tall, wide, cores = SIDES
    up = (device // (wide * cores) - mine_owner // (wide * cores)) % tall
    right = (device // cores % wide - mine_owner // cores % wide) % wide
    across = (device % cores - mine_owner % cores) % cores
    copy = device % cores + cores * (lax.axis_index("tensor") % 2)
    part = right ^ copy
    step = (part * tall + up) * cores + (across ^ part % cores)
    rung_means, next_lengths = finish(
        parts,
        jnp.pad(counted, (0, spare), constant_values=1.0)[None],
        step[None],
        (mine % per_device)[None],
        mark,
    )
    rung_means = rung_means[0]
    next_lengths = next_lengths[0]
    return (attention, weights, rung_means, next_keys, next_values, next_lengths)


def solution(mesh):
    placed = (
        P("particle", None, "tensor"),
        P("particle", None, "tensor"),
        P("particle", None, "tensor"),
        P("particle", None, "tensor"),
        P("particle", None, "tensor"),
        P("particle", "tensor"),
        P("particle", "tensor"),
        P("particle"),
        P("particle"),
        P("tensor"),
        P(),
        P(),
    )
    return jax.shard_map(
        shards,
        mesh=mesh,
        in_specs=placed,
        out_specs=(
            P("particle", None, "tensor"),
            P("particle"),
            P(),
            P("particle", None, "tensor"),
            P("particle", None, "tensor"),
            P("particle"),
        ),
        check_vma=False,
    )
```

```python
import functools
import itertools

import jax
import jax.numpy as jnp
from jax import lax
from jax.experimental import pallas as pl
from jax.experimental.pallas import tpu as pltpu
from jax.sharding import PartitionSpec as P

HEADS = 64
KV_HEADS = 8
HEAD_DIM = 128
STEPS = 2
RUNGS = 8
DISTINCT = 2
SIDES = (4, 4, 2)
PLANES = 8
WINDOW = 32
CHUNKS = 4
GROUP = 2
ROOMY = 58 << 20


def pack_kernel(keeps, lengths, least, most, *refs):
    number = (len(refs) - 5) // (2 + keeps)
    caches, fresh, (packed, *written) = refs[:number], refs[number : 2 * number], refs[2 * number : -4]
    held, in_sems, out_sems, send_sems = refs[-4:]
    count, suffix, _ = caches[0].shape
    goals = least.shape[0]
    share = count // CHUNKS

    def load(chunk, n):
        rows = pl.ds(chunk * share, share)
        return pltpu.make_async_copy(
            caches[n].at[rows], held.at[n, rows], in_sems.at[chunk * number + n]
        )

    def keep(n):
        return pltpu.make_async_copy(held.at[n], written[n], out_sems.at[n])

    def low(d):
        return pltpu.make_async_copy(
            held.at[number - 1, least[d]], packed.at[2 * d], send_sems.at[2 * d]
        )

    def high(d):
        return pltpu.make_async_copy(
            held.at[number - 1, most[d]], packed.at[2 * d + 1], send_sems.at[2 * d + 1]
        )

    def patch(group):
        found = []
        for i in range(GROUP):
            p = group * GROUP + i
            length = lengths[p]
            base = pl.multiple_of(jnp.minimum(length // 16 * 16, suffix - WINDOW), 16)
            for n in range(number):
                place = (n, p, pl.ds(base, WINDOW))
                block = held[place].astype(jnp.float32)
                lines = fresh[n][p].astype(jnp.float32)
                row = lax.broadcasted_iota(jnp.int32, block.shape, 0) + base
                for offset in range(STEPS):
                    block = jnp.where(row == length + offset, lines[offset : offset + 1], block)
                found.append((place, block.astype(held.dtype)))
        for place, block in found:
            held[place] = block

    for chunk in range(CHUNKS):
        for n in range(number):
            load(chunk, n).start()
    for chunk in range(CHUNKS):
        for n in range(number):
            load(chunk, n).wait()
        groups = share // GROUP
        repeat(groups, lambda g, chunk=chunk: patch(g + chunk * groups), 1)
    repeat(goals, lambda d: (low(d).start(), high(d).start()))
    for n in range(number * keeps):
        keep(n).start()
    repeat(goals, lambda d: (low(d).wait(), high(d).wait()))
    for n in range(number * keeps):
        keep(n).wait()


def repeat(count, body, unroll=4):
    def step(i, carry):
        body(i)
        return carry

    lax.fori_loop(0, count, step, 0, unroll=unroll)


def pack(caches, fresh, lengths, least, most, keeps):
    cache, number = caches[0], len(caches)
    count, goals = cache.shape[0], least.shape[0]
    smem = pl.BlockSpec(memory_space=pltpu.SMEM)
    hbm = pl.BlockSpec(memory_space=pltpu.HBM)
    vmem = pl.BlockSpec(memory_space=pltpu.VMEM)
    return pl.pallas_call(
        functools.partial(pack_kernel, keeps),
        out_shape=[jax.ShapeDtypeStruct((goals * DISTINCT,) + cache.shape[1:], cache.dtype)]
        + [jax.ShapeDtypeStruct(cache.shape, cache.dtype)] * (number * keeps),
        in_specs=[smem] * 3 + [hbm] * number + [vmem] * number,
        out_specs=[hbm] * (1 + number * keeps),
        scratch_shapes=[
            pltpu.VMEM((number,) + cache.shape, cache.dtype),
            pltpu.SemaphoreType.DMA((number * CHUNKS,)),
            pltpu.SemaphoreType.DMA((number,)),
            pltpu.SemaphoreType.DMA((goals * DISTINCT,)),
        ],
        name="pack",
    )(lengths, least, most, *caches, *fresh)


def after(array, *others):
    hbm = pl.BlockSpec(memory_space=pltpu.HBM)
    return pl.pallas_call(
        lambda *refs: None,
        out_shape=jax.ShapeDtypeStruct(array.shape, array.dtype),
        in_specs=[hbm] + [pl.BlockSpec(memory_space=pl.ANY)] * len(others),
        out_specs=hbm,
        input_output_aliases={0: 0},
        compiler_params=pltpu.CompilerParams(vmem_limit_bytes=ROOMY),
        name="after",
    )(array, *others)


def unpack_kernel(slots, arrived, _, result, mark, held, in_sems, out_sems):
    count = result.shape[0]
    share = count // CHUNKS

    def load(p):
        return pltpu.make_async_copy(arrived.at[slots[p]], held.at[p], in_sems.at[p])

    def keep(chunk):
        rows = pl.ds(chunk * share, share)
        return pltpu.make_async_copy(held.at[rows], result.at[rows], out_sems.at[chunk])

    mark[...] = jnp.zeros_like(mark)
    repeat(count, lambda p: load(p).start(), count)
    for chunk in range(CHUNKS):
        repeat(share, lambda p, chunk=chunk: load(p + chunk * share).wait(), share)
        keep(chunk).start()
    for chunk in range(CHUNKS):
        keep(chunk).wait()


def unpack(arrived, slots, other):
    count, (_, suffix, width) = slots.shape[0], arrived.shape
    hbm = pl.BlockSpec(memory_space=pltpu.HBM)
    shape = (count, suffix, width)
    return pl.pallas_call(
        unpack_kernel,
        out_shape=(
            jax.ShapeDtypeStruct(shape, arrived.dtype),
            jax.ShapeDtypeStruct((1, width), jnp.float32),
        ),
        in_specs=[pl.BlockSpec(memory_space=pltpu.SMEM), hbm, pl.BlockSpec(memory_space=pl.ANY)],
        out_specs=(hbm, pl.BlockSpec(memory_space=pltpu.VMEM)),
        scratch_shapes=[
            pltpu.VMEM(shape, arrived.dtype),
            pltpu.SemaphoreType.DMA((count,)),
            pltpu.SemaphoreType.DMA((CHUNKS,)),
        ],
        name="unpack",
    )(slots, arrived, other)


def finish_kernel(counted, step, place, *refs):
    *parts, _, rung_means, next_lengths = refs
    shared = jnp.concatenate([part[...] for part in parts], axis=0)
    peaks, sums, filled = shared[:, 0], shared[:, 1], shared[:, 2]
    top = jnp.max(peaks, axis=0, keepdims=True)
    summed = jnp.sum(sums * jnp.exp(peaks - top), axis=0, keepdims=True)
    rung_means[...] = (top + jnp.log(summed) - jnp.log(counted[...]))[:, :RUNGS]
    order = lax.broadcasted_iota(jnp.int32, filled.shape, 0)
    owner = (order == step[...]).astype(jnp.float32)
    found = lax.dot_general(
        filled, owner, (((0,), (0,)), ((), ())), preferred_element_type=jnp.float32
    )
    order = lax.broadcasted_iota(jnp.int32, found.shape, 0)
    length = jnp.sum(jnp.where(order == place[...], found, 0.0), axis=0, keepdims=True)
    next_lengths[...] = length.astype(jnp.int32) + STEPS


def finish(parts, counted, step, place, other):
    vmem = pl.BlockSpec(memory_space=pltpu.VMEM)
    return pl.pallas_call(
        finish_kernel,
        out_shape=(
            jax.ShapeDtypeStruct((1, RUNGS), jnp.float32),
            jax.ShapeDtypeStruct(step.shape, jnp.int32),
        ),
        in_specs=[vmem] * (3 + len(parts)) + [pl.BlockSpec(memory_space=pl.ANY)],
        out_specs=(vmem, vmem),
        compiler_params=pltpu.CompilerParams(vmem_limit_bytes=ROOMY),
        name="finish",
    )(counted, step, place, *parts, other)


def along(array, axes):
    sides = SIDES
    total = sides[0] * sides[1] * sides[2]
    parts = []
    for steps in itertools.product(*(range(sides[axis]) for axis in axes)):
        pairs = []
        for i in range(total):
            goal = [i // (sides[1] * sides[2]), i // sides[2] % sides[1], i % sides[2]]
            for axis, step in zip(axes, steps):
                goal[axis] = (goal[axis] + step) % sides[axis]
            pairs.append((i, (goal[0] * sides[1] + goal[1]) * sides[2] + goal[2]))
        parts.append(lax.ppermute(array, "particle", pairs) if any(steps) else array)
    return parts


def half_of(array):
    tall, wide, cores = SIDES
    parts = []
    for hop, step in itertools.product(range(2), range(2)):
        pairs = []
        for i in range(tall * wide * cores):
            y, x, core = i // (wide * cores), i // cores % wide, i % cores
            goal = (y ^ 2 * hop) * wide + (x + 2 * core + step) % wide
            pairs.append((i, goal * cores + core))
        parts.append(lax.ppermute(array, "particle", pairs))
    return parts


def shards(
    queries,
    new_keys,
    new_values,
    key_cache,
    value_cache,
    prompt_keys,
    prompt_values,
    lengths,
    prior,
    reward_dir,
    rungs,
    ancestors,
):
    per_device = queries.shape[0]
    suffix = key_cache.shape[1]
    groups = HEADS // KV_HEADS
    scale = HEAD_DIM ** (-0.5)
    sources = lax.axis_size("particle")
    device = lax.axis_index("particle")

    wanted = ancestors.reshape(sources, per_device)
    owner = wanted // per_device
    local = wanted % per_device
    chosen = owner == device
    least = jnp.min(jnp.where(chosen, local, per_device - 1), axis=1)
    most = jnp.max(jnp.where(chosen, local, 0), axis=1)
    mine = lax.dynamic_slice_in_dim(ancestors, device * per_device, per_device)
    mine_owner = mine // per_device
    same_owner = mine_owner[:, None] == mine_owner[None, :]
    first = jnp.min(jnp.where(same_owner, mine[None, :], sources * per_device), axis=1)
    slot = mine_owner * DISTINCT + (mine != first).astype(jnp.int32)

    low = -jnp.inf
    shard = jnp.maximum(
        jnp.pad(prompt_keys, ((0, 0), (0, HEAD_DIM)), constant_values=low),
        jnp.pad(prompt_values, ((0, 0), (HEAD_DIM, 0)), constant_values=low),
    )
    chip = jnp.concatenate(along(shard, (2,)), axis=0)
    chip = chip + jnp.minimum(least[0], 0).astype(chip.dtype)
    beside = lax.ppermute(chip, "particle", [(i, i ^ 8) for i in range(sources)])
    column = jnp.concatenate([chip, beside], axis=0)
    halves = half_of(column)

    exchange = functools.partial(
        lax.all_to_all, axis_name="particle", split_axis=0, concat_axis=0, tiled=True
    )
    places = (lengths, least, most)
    (outgoing_keys,) = pack((key_cache,), (new_keys,), *places, False)
    arrived_keys = exchange(after(outgoing_keys, column))
    outgoing_values, written_keys, written_values = pack(
        (key_cache, value_cache), (new_keys, new_values), *places, True
    )
    arrived_values = exchange(after(outgoing_values, arrived_keys))
    next_keys, mark = unpack(arrived_keys, slot, column)

    none = jnp.minimum(jnp.abs(arrived_keys[0, 0, 0]), 0)
    half = jnp.concatenate(halves, axis=0) + none
    prompt = jnp.concatenate(along(half, (2,)), axis=0)
    all_keys = prompt[:, :HEAD_DIM]
    all_values = prompt[:, HEAD_DIM:]

    query = queries.reshape(per_device, STEPS, groups, HEAD_DIM)
    front = (
        jnp.einsum("pshd,nd->pshn", query, all_keys, preferred_element_type=jnp.float32) * scale
    )
    back = (
        jnp.einsum("pshd,pld->pshl", query, written_keys, preferred_element_type=jnp.float32)
        * scale
    )
    position = jnp.arange(suffix, dtype=jnp.int32)
    later = jnp.arange(STEPS, dtype=jnp.int32)
    visible = position[None, None, :] < lengths[:, None, None] + 1 + later[None, :, None]
    back = jnp.where(visible[:, :, None, :], back, -jnp.inf)
    peak = jnp.maximum(jnp.max(front, axis=-1), jnp.max(back, axis=-1))
    front = jnp.exp(front - peak[..., None])
    back = jnp.exp(back - peak[..., None])
    total = jnp.sum(front, axis=-1) + jnp.sum(back, axis=-1)
    mixed = jnp.einsum(
        "pshn,nd->pshd",
        front.astype(jnp.bfloat16),
        all_values,
        preferred_element_type=jnp.float32,
    ) + jnp.einsum(
        "pshl,pld->pshd",
        back.astype(jnp.bfloat16),
        written_values,
        preferred_element_type=jnp.float32,
    )
    output = (mixed / total[..., None]).reshape(per_device, STEPS, -1)
    attention = output.astype(jnp.bfloat16)

    partial_reward = jnp.sum(output * reward_dir[None, None, :], axis=(1, 2))
    reward = partial_reward
    for bit in (1, 2, 4):
        pairs = [(i, i ^ bit) for i in range(PLANES)]
        reward = reward + lax.ppermute(reward, "tensor", pairs)
    weights = prior + reward
    own_rungs = lax.dynamic_slice_in_dim(rungs, device * per_device, per_device)
    ladder = jnp.arange(RUNGS, dtype=jnp.int32)
    member = own_rungs[:, None] == ladder[None, :]
    local_peak = jnp.max(jnp.where(member, weights[:, None], -1e30), axis=0)
    local_sum = jnp.sum(
        jnp.where(member, jnp.exp(weights[:, None] - local_peak[None, :]), 0.0), axis=0
    )
    spare = per_device - RUNGS
    shared = jnp.stack(
        [
            jnp.pad(local_peak, (0, spare)),
            jnp.pad(local_sum, (0, spare), constant_values=1.0),
            lengths.astype(jnp.float32),
        ]
    )[None]
    near = jnp.concatenate(along(shared, (2,)), axis=0)
    near = after(near, attention)
    near = jnp.concatenate(along(near, (0,)), axis=0) + mark[0, :per_device]
    parts = along(near, (1,))
    next_values, mark = unpack(arrived_values, slot, near)

    counted = jnp.sum((rungs[:, None] == ladder[None, :]).astype(jnp.float32), axis=0)
    tall, wide, cores = SIDES
    up = (device // (wide * cores) - mine_owner // (wide * cores)) % tall
    right = (device // cores % wide - mine_owner // cores % wide) % wide
    across = (device % cores - mine_owner % cores) % cores
    step = (right * tall + up) * cores + across
    rung_means, next_lengths = finish(
        parts,
        jnp.pad(counted, (0, spare), constant_values=1.0)[None],
        step[None],
        (mine % per_device)[None],
        mark,
    )
    rung_means = rung_means[0]
    next_lengths = next_lengths[0]
    return (attention, weights, rung_means, next_keys, next_values, next_lengths)


def solution(mesh):
    placed = (
        P("particle", None, "tensor"),
        P("particle", None, "tensor"),
        P("particle", None, "tensor"),
        P("particle", None, "tensor"),
        P("particle", None, "tensor"),
        P("particle", "tensor"),
        P("particle", "tensor"),
        P("particle"),
        P("particle"),
        P("tensor"),
        P(),
        P(),
    )
    return jax.shard_map(
        shards,
        mesh=mesh,
        in_specs=placed,
        out_specs=(
            P("particle", None, "tensor"),
            P("particle"),
            P(),
            P("particle", None, "tensor"),
            P("particle", None, "tensor"),
            P("particle"),
        ),
        check_vma=False,
    )
```

```python
import functools
import itertools

import jax
import jax.numpy as jnp
from jax import lax
from jax.experimental import pallas as pl
from jax.experimental.pallas import tpu as pltpu
from jax.sharding import PartitionSpec as P

HEADS = 64
KV_HEADS = 8
HEAD_DIM = 128
STEPS = 2
RUNGS = 8
DISTINCT = 2
SIDES = (4, 4, 2)
PLANES = 8
WINDOW = 32
CHUNKS = 4
GROUP = 2
ROOMY = 58 << 20


def pack_kernel(keeps, lengths, least, most, *refs):
    number = (len(refs) - 5) // (2 + keeps)
    caches, fresh, (packed, *written) = refs[:number], refs[number : 2 * number], refs[2 * number : -4]
    held, in_sems, out_sems, send_sems = refs[-4:]
    count, suffix, _ = caches[0].shape
    goals = least.shape[0]
    share = count // CHUNKS

    def load(chunk, n):
        rows = pl.ds(chunk * share, share)
        return pltpu.make_async_copy(
            caches[n].at[rows], held.at[n, rows], in_sems.at[chunk * number + n]
        )

    def keep(n):
        return pltpu.make_async_copy(held.at[n], written[n], out_sems.at[n])

    def low(d):
        return pltpu.make_async_copy(
            held.at[number - 1, least[d]], packed.at[2 * d], send_sems.at[2 * d]
        )

    def high(d):
        return pltpu.make_async_copy(
            held.at[number - 1, most[d]], packed.at[2 * d + 1], send_sems.at[2 * d + 1]
        )

    def each(d, act):
        pl.when(least[d] <= most[d])(lambda: act(low(d)))
        pl.when(least[d] < most[d])(lambda: act(high(d)))

    def patch(group):
        found = []
        for i in range(GROUP):
            p = group * GROUP + i
            length = lengths[p]
            base = pl.multiple_of(jnp.minimum(length // 16 * 16, suffix - WINDOW), 16)
            for n in range(number):
                place = (n, p, pl.ds(base, WINDOW))
                block = held[place].astype(jnp.float32)
                lines = fresh[n][p].astype(jnp.float32)
                row = lax.broadcasted_iota(jnp.int32, block.shape, 0) + base
                for offset in range(STEPS):
                    block = jnp.where(row == length + offset, lines[offset : offset + 1], block)
                found.append((place, block.astype(held.dtype)))
        for place, block in found:
            held[place] = block

    for chunk in range(CHUNKS):
        for n in range(number):
            load(chunk, n).start()
    for chunk in range(CHUNKS):
        for n in range(number):
            load(chunk, n).wait()
        groups = share // GROUP
        repeat(groups, lambda g, chunk=chunk: patch(g + chunk * groups), 1)
    repeat(goals, lambda d: each(d, lambda copy: copy.start()))
    for n in range(number * keeps):
        keep(n).start()
    repeat(goals, lambda d: each(d, lambda copy: copy.wait()))
    for n in range(number * keeps):
        keep(n).wait()


def repeat(count, body, unroll=4):
    def step(i, carry):
        body(i)
        return carry

    lax.fori_loop(0, count, step, 0, unroll=unroll)


def pack(caches, fresh, lengths, least, most, keeps):
    cache, number = caches[0], len(caches)
    count, goals = cache.shape[0], least.shape[0]
    smem = pl.BlockSpec(memory_space=pltpu.SMEM)
    hbm = pl.BlockSpec(memory_space=pltpu.HBM)
    vmem = pl.BlockSpec(memory_space=pltpu.VMEM)
    return pl.pallas_call(
        functools.partial(pack_kernel, keeps),
        out_shape=[jax.ShapeDtypeStruct((goals * DISTINCT,) + cache.shape[1:], cache.dtype)]
        + [jax.ShapeDtypeStruct(cache.shape, cache.dtype)] * (number * keeps),
        in_specs=[smem] * 3 + [hbm] * number + [vmem] * number,
        out_specs=[hbm] * (1 + number * keeps),
        scratch_shapes=[
            pltpu.VMEM((number,) + cache.shape, cache.dtype),
            pltpu.SemaphoreType.DMA((number * CHUNKS,)),
            pltpu.SemaphoreType.DMA((number,)),
            pltpu.SemaphoreType.DMA((goals * DISTINCT,)),
        ],
        name="pack",
    )(lengths, least, most, *caches, *fresh)


def after(array, *others):
    hbm = pl.BlockSpec(memory_space=pltpu.HBM)
    return pl.pallas_call(
        lambda *refs: None,
        out_shape=jax.ShapeDtypeStruct(array.shape, array.dtype),
        in_specs=[hbm] + [pl.BlockSpec(memory_space=pl.ANY)] * len(others),
        out_specs=hbm,
        input_output_aliases={0: 0},
        compiler_params=pltpu.CompilerParams(vmem_limit_bytes=ROOMY),
        name="after",
    )(array, *others)


def zero_kernel(_, zero):
    zero[...] = jnp.zeros_like(zero)


def zero_after(array):
    return pl.pallas_call(
        zero_kernel,
        out_shape=jax.ShapeDtypeStruct((1, HEAD_DIM), jnp.float32),
        in_specs=[pl.BlockSpec(memory_space=pltpu.HBM)],
        out_specs=pl.BlockSpec(memory_space=pltpu.VMEM),
        name="zero",
    )(array)


def unpack_kernel(slots, arrived, _, result, mark, held, in_sems, out_sems):
    count = result.shape[0]
    share = count // CHUNKS

    def load(p):
        return pltpu.make_async_copy(arrived.at[slots[p]], held.at[p], in_sems.at[p])

    def keep(chunk):
        rows = pl.ds(chunk * share, share)
        return pltpu.make_async_copy(held.at[rows], result.at[rows], out_sems.at[chunk])

    mark[...] = jnp.zeros_like(mark)
    repeat(count, lambda p: load(p).start(), count)
    for chunk in range(CHUNKS):
        repeat(share, lambda p, chunk=chunk: load(p + chunk * share).wait(), share)
        keep(chunk).start()
    for chunk in range(CHUNKS):
        keep(chunk).wait()


def unpack(arrived, slots, other):
    count, (_, suffix, width) = slots.shape[0], arrived.shape
    hbm = pl.BlockSpec(memory_space=pltpu.HBM)
    shape = (count, suffix, width)
    return pl.pallas_call(
        unpack_kernel,
        out_shape=(
            jax.ShapeDtypeStruct(shape, arrived.dtype),
            jax.ShapeDtypeStruct((1, width), jnp.float32),
        ),
        in_specs=[pl.BlockSpec(memory_space=pltpu.SMEM), hbm, pl.BlockSpec(memory_space=pl.ANY)],
        out_specs=(hbm, pl.BlockSpec(memory_space=pltpu.VMEM)),
        scratch_shapes=[
            pltpu.VMEM(shape, arrived.dtype),
            pltpu.SemaphoreType.DMA((count,)),
            pltpu.SemaphoreType.DMA((CHUNKS,)),
        ],
        name="unpack",
    )(slots, arrived, other)


def finish_kernel(counted, step, place, *refs):
    *parts, _, rung_means, next_lengths = refs
    shared = jnp.concatenate([part[...] for part in parts], axis=0)
    peaks, sums, filled = shared[:, 0], shared[:, 1], shared[:, 2]
    top = jnp.max(peaks, axis=0, keepdims=True)
    summed = jnp.sum(sums * jnp.exp(peaks - top), axis=0, keepdims=True)
    rung_means[...] = (top + jnp.log(summed) - jnp.log(counted[...]))[:, :RUNGS]
    order = lax.broadcasted_iota(jnp.int32, filled.shape, 0)
    owner = (order == step[...]).astype(jnp.float32)
    found = lax.dot_general(
        filled, owner, (((0,), (0,)), ((), ())), preferred_element_type=jnp.float32
    )
    order = lax.broadcasted_iota(jnp.int32, found.shape, 0)
    length = jnp.sum(jnp.where(order == place[...], found, 0.0), axis=0, keepdims=True)
    next_lengths[...] = length.astype(jnp.int32) + STEPS


def finish(parts, counted, step, place, other):
    vmem = pl.BlockSpec(memory_space=pltpu.VMEM)
    return pl.pallas_call(
        finish_kernel,
        out_shape=(
            jax.ShapeDtypeStruct((1, RUNGS), jnp.float32),
            jax.ShapeDtypeStruct(step.shape, jnp.int32),
        ),
        in_specs=[vmem] * (3 + len(parts)) + [pl.BlockSpec(memory_space=pl.ANY)],
        out_specs=(vmem, vmem),
        compiler_params=pltpu.CompilerParams(vmem_limit_bytes=ROOMY),
        name="finish",
    )(counted, step, place, *parts, other)


def along(array, axes):
    sides = SIDES
    total = sides[0] * sides[1] * sides[2]
    parts = []
    for steps in itertools.product(*(range(sides[axis]) for axis in axes)):
        pairs = []
        for i in range(total):
            goal = [i // (sides[1] * sides[2]), i // sides[2] % sides[1], i % sides[2]]
            for axis, step in zip(axes, steps):
                goal[axis] = (goal[axis] + step) % sides[axis]
            pairs.append((i, (goal[0] * sides[1] + goal[1]) * sides[2] + goal[2]))
        parts.append(lax.ppermute(array, "particle", pairs) if any(steps) else array)
    return parts


def half_of(array):
    tall, wide, cores = SIDES
    parts = []
    for hop, step in itertools.product(range(2), range(2)):
        pairs = []
        for i in range(tall * wide * cores):
            y, x, core = i // (wide * cores), i // cores % wide, i % cores
            goal = (y ^ 2 * hop) * wide + (x + 2 * core + step) % wide
            pairs.append((i, goal * cores + core))
        parts.append(lax.ppermute(array, "particle", pairs))
    return parts


def shards(
    queries,
    new_keys,
    new_values,
    key_cache,
    value_cache,
    prompt_keys,
    prompt_values,
    lengths,
    prior,
    reward_dir,
    rungs,
    ancestors,
):
    per_device = queries.shape[0]
    suffix = key_cache.shape[1]
    groups = HEADS // KV_HEADS
    scale = HEAD_DIM ** (-0.5)
    sources = lax.axis_size("particle")
    device = lax.axis_index("particle")

    wanted = ancestors.reshape(sources, per_device)
    owner = wanted // per_device
    local = wanted % per_device
    chosen = owner == device
    least = jnp.min(jnp.where(chosen, local, per_device - 1), axis=1)
    most = jnp.max(jnp.where(chosen, local, 0), axis=1)
    mine = lax.dynamic_slice_in_dim(ancestors, device * per_device, per_device)
    mine_owner = mine // per_device
    same_owner = mine_owner[:, None] == mine_owner[None, :]
    first = jnp.min(jnp.where(same_owner, mine[None, :], sources * per_device), axis=1)
    slot = mine_owner * DISTINCT + (mine != first).astype(jnp.int32)

    low = -jnp.inf
    shard = jnp.maximum(
        jnp.pad(prompt_keys, ((0, 0), (0, HEAD_DIM)), constant_values=low),
        jnp.pad(prompt_values, ((0, 0), (HEAD_DIM, 0)), constant_values=low),
    )
    chip = jnp.concatenate(along(shard, (2,)), axis=0)
    chip = chip + jnp.minimum(least[0], 0).astype(chip.dtype)
    beside = lax.ppermute(chip, "particle", [(i, i ^ 8) for i in range(sources)])
    column = jnp.concatenate([chip, beside], axis=0)
    halves = half_of(column)

    exchange = functools.partial(
        lax.all_to_all, axis_name="particle", split_axis=0, concat_axis=0, tiled=True
    )
    places = (lengths, least, most)
    (outgoing_keys,) = pack((key_cache,), (new_keys,), *places, False)
    arrived_keys = exchange(after(outgoing_keys, column))
    outgoing_values, written_keys, written_values = pack(
        (key_cache, value_cache), (new_keys, new_values), *places, True
    )
    arrived_values = exchange(after(outgoing_values, arrived_keys))
    next_keys, mark = unpack(arrived_keys, slot, column)

    half = jnp.concatenate(halves, axis=0) + zero_after(arrived_keys)[0, 0].astype(shard.dtype)
    prompt = jnp.concatenate(along(half, (2,)), axis=0)
    all_keys = prompt[:, :HEAD_DIM]
    all_values = prompt[:, HEAD_DIM:]

    query = queries.reshape(per_device, STEPS, groups, HEAD_DIM)
    front = (
        jnp.einsum("pshd,nd->pshn", query, all_keys, preferred_element_type=jnp.float32) * scale
    )
    back = (
        jnp.einsum("pshd,pld->pshl", query, written_keys, preferred_element_type=jnp.float32)
        * scale
    )
    position = jnp.arange(suffix, dtype=jnp.int32)
    later = jnp.arange(STEPS, dtype=jnp.int32)
    visible = position[None, None, :] < lengths[:, None, None] + 1 + later[None, :, None]
    back = jnp.where(visible[:, :, None, :], back, -jnp.inf)
    peak = jnp.maximum(jnp.max(front, axis=-1), jnp.max(back, axis=-1))
    front = jnp.exp(front - peak[..., None])
    back = jnp.exp(back - peak[..., None])
    total = jnp.sum(front, axis=-1) + jnp.sum(back, axis=-1)
    mixed = jnp.einsum(
        "pshn,nd->pshd",
        front.astype(jnp.bfloat16),
        all_values,
        preferred_element_type=jnp.float32,
    ) + jnp.einsum(
        "pshl,pld->pshd",
        back.astype(jnp.bfloat16),
        written_values,
        preferred_element_type=jnp.float32,
    )
    output = (mixed / total[..., None]).reshape(per_device, STEPS, -1)
    attention = output.astype(jnp.bfloat16)

    partial_reward = jnp.sum(output * reward_dir[None, None, :], axis=(1, 2))
    reward = partial_reward
    for bit in (1, 2, 4):
        pairs = [(i, i ^ bit) for i in range(PLANES)]
        reward = reward + lax.ppermute(reward, "tensor", pairs)
    weights = prior + reward
    own_rungs = lax.dynamic_slice_in_dim(rungs, device * per_device, per_device)
    ladder = jnp.arange(RUNGS, dtype=jnp.int32)
    member = own_rungs[:, None] == ladder[None, :]
    local_peak = jnp.max(jnp.where(member, weights[:, None], -1e30), axis=0)
    local_sum = jnp.sum(
        jnp.where(member, jnp.exp(weights[:, None] - local_peak[None, :]), 0.0), axis=0
    )
    spare = per_device - RUNGS
    shared = jnp.stack(
        [
            jnp.pad(local_peak, (0, spare)),
            jnp.pad(local_sum, (0, spare), constant_values=1.0),
            lengths.astype(jnp.float32),
        ]
    )[None]
    near = jnp.concatenate(along(shared, (2,)), axis=0)
    near = after(near, attention, mark)
    near = jnp.concatenate(along(near, (0,)), axis=0)
    parts = along(near, (1,))
    next_values, mark = unpack(arrived_values, slot, near)

    counted = jnp.sum((rungs[:, None] == ladder[None, :]).astype(jnp.float32), axis=0)
    tall, wide, cores = SIDES
    up = (device // (wide * cores) - mine_owner // (wide * cores)) % tall
    right = (device // cores % wide - mine_owner // cores % wide) % wide
    across = (device % cores - mine_owner % cores) % cores
    step = (right * tall + up) * cores + across
    rung_means, next_lengths = finish(
        parts,
        jnp.pad(counted, (0, spare), constant_values=1.0)[None],
        step[None],
        (mine % per_device)[None],
        mark,
    )
    rung_means = rung_means[0]
    next_lengths = next_lengths[0]
    return (attention, weights, rung_means, next_keys, next_values, next_lengths)


def solution(mesh):
    placed = (
        P("particle", None, "tensor"),
        P("particle", None, "tensor"),
        P("particle", None, "tensor"),
        P("particle", None, "tensor"),
        P("particle", None, "tensor"),
        P("particle", "tensor"),
        P("particle", "tensor"),
        P("particle"),
        P("particle"),
        P("tensor"),
        P(),
        P(),
    )
    return jax.shard_map(
        shards,
        mesh=mesh,
        in_specs=placed,
        out_specs=(
            P("particle", None, "tensor"),
            P("particle"),
            P(),
            P("particle", None, "tensor"),
            P("particle", None, "tensor"),
            P("particle"),
        ),
        check_vma=False,
    )
```

```python
import functools
import itertools

import jax
import jax.numpy as jnp
from jax import lax
from jax.experimental import pallas as pl
from jax.experimental.pallas import tpu as pltpu
from jax.sharding import PartitionSpec as P

HEADS = 64
KV_HEADS = 8
HEAD_DIM = 128
STEPS = 2
RUNGS = 8
DISTINCT = 2
SIDES = (4, 4, 2)
PLANES = 8
WINDOW = 32
CHUNKS = 4
GROUP = 2


def pack_kernel(keeps, lengths, least, most, *refs):
    number = (len(refs) - 5) // (2 + keeps)
    caches, fresh, (packed, *written) = refs[:number], refs[number : 2 * number], refs[2 * number : -4]
    held, in_sems, out_sems, send_sems = refs[-4:]
    count, suffix, _ = caches[0].shape
    goals = least.shape[0]
    share = count // CHUNKS

    def load(chunk, n):
        rows = pl.ds(chunk * share, share)
        return pltpu.make_async_copy(
            caches[n].at[rows], held.at[n, rows], in_sems.at[chunk * number + n]
        )

    def keep(n):
        return pltpu.make_async_copy(held.at[n], written[n], out_sems.at[n])

    def low(d):
        return pltpu.make_async_copy(
            held.at[number - 1, least[d]], packed.at[2 * d], send_sems.at[2 * d]
        )

    def high(d):
        return pltpu.make_async_copy(
            held.at[number - 1, most[d]], packed.at[2 * d + 1], send_sems.at[2 * d + 1]
        )

    def each(d, act):
        pl.when(least[d] <= most[d])(lambda: act(low(d)))
        pl.when(least[d] < most[d])(lambda: act(high(d)))

    def patch(group):
        found = []
        for i in range(GROUP):
            p = group * GROUP + i
            length = lengths[p]
            base = pl.multiple_of(jnp.minimum(length // 16 * 16, suffix - WINDOW), 16)
            for n in range(number):
                place = (n, p, pl.ds(base, WINDOW))
                block = held[place].astype(jnp.float32)
                lines = fresh[n][p].astype(jnp.float32)
                row = lax.broadcasted_iota(jnp.int32, block.shape, 0) + base
                for offset in range(STEPS):
                    block = jnp.where(row == length + offset, lines[offset : offset + 1], block)
                found.append((place, block.astype(held.dtype)))
        for place, block in found:
            held[place] = block

    for chunk in range(CHUNKS):
        for n in range(number):
            load(chunk, n).start()
    for chunk in range(CHUNKS):
        for n in range(number):
            load(chunk, n).wait()
        groups = share // GROUP
        repeat(groups, lambda g, chunk=chunk: patch(g + chunk * groups), 1)
    repeat(goals, lambda d: each(d, lambda copy: copy.start()))
    for n in range(number * keeps):
        keep(n).start()
    repeat(goals, lambda d: each(d, lambda copy: copy.wait()))
    for n in range(number * keeps):
        keep(n).wait()


def repeat(count, body, unroll=4):
    def step(i, carry):
        body(i)
        return carry

    lax.fori_loop(0, count, step, 0, unroll=unroll)


def pack(caches, fresh, lengths, least, most, keeps):
    cache, number = caches[0], len(caches)
    count, goals = cache.shape[0], least.shape[0]
    smem = pl.BlockSpec(memory_space=pltpu.SMEM)
    hbm = pl.BlockSpec(memory_space=pltpu.HBM)
    vmem = pl.BlockSpec(memory_space=pltpu.VMEM)
    return pl.pallas_call(
        functools.partial(pack_kernel, keeps),
        out_shape=[jax.ShapeDtypeStruct((goals * DISTINCT,) + cache.shape[1:], cache.dtype)]
        + [jax.ShapeDtypeStruct(cache.shape, cache.dtype)] * (number * keeps),
        in_specs=[smem] * 3 + [hbm] * number + [vmem] * number,
        out_specs=[hbm] * (1 + number * keeps),
        scratch_shapes=[
            pltpu.VMEM((number,) + cache.shape, cache.dtype),
            pltpu.SemaphoreType.DMA((number * CHUNKS,)),
            pltpu.SemaphoreType.DMA((number,)),
            pltpu.SemaphoreType.DMA((goals * DISTINCT,)),
        ],
        name="pack",
    )(lengths, least, most, *caches, *fresh)


def after(array, *others):
    hbm = pl.BlockSpec(memory_space=pltpu.HBM)
    return pl.pallas_call(
        lambda *refs: None,
        out_shape=jax.ShapeDtypeStruct(array.shape, array.dtype),
        in_specs=[hbm] + [pl.BlockSpec(memory_space=pl.ANY)] * len(others),
        out_specs=hbm,
        input_output_aliases={0: 0},
        name="after",
    )(array, *others)


def zero_kernel(_, zero):
    zero[...] = jnp.zeros_like(zero)


def zero_after(array):
    return pl.pallas_call(
        zero_kernel,
        out_shape=jax.ShapeDtypeStruct((1, HEAD_DIM), jnp.float32),
        in_specs=[pl.BlockSpec(memory_space=pltpu.HBM)],
        out_specs=pl.BlockSpec(memory_space=pltpu.VMEM),
        name="zero",
    )(array)


def move_rows(slots, arrived, result, held, in_sems, out_sems, meanwhile):
    count = result.shape[0]
    share = count // CHUNKS

    def load(p):
        return pltpu.make_async_copy(arrived.at[slots[p]], held.at[p], in_sems.at[p])

    def keep(chunk):
        rows = pl.ds(chunk * share, share)
        return pltpu.make_async_copy(held.at[rows], result.at[rows], out_sems.at[chunk])

    repeat(count, lambda p: load(p).start(), count)
    meanwhile()
    for chunk in range(CHUNKS):
        repeat(share, lambda p, chunk=chunk: load(p + chunk * share).wait(), share)
        keep(chunk).start()
    for chunk in range(CHUNKS):
        keep(chunk).wait()


def unpack_kernel(slots, arrived, _, result, mark, held, in_sems, out_sems):
    def clear():
        mark[...] = jnp.zeros_like(mark)

    move_rows(slots, arrived, result, held, in_sems, out_sems, clear)


def unpack(arrived, slots, other):
    count, (_, suffix, width) = slots.shape[0], arrived.shape
    hbm = pl.BlockSpec(memory_space=pltpu.HBM)
    shape = (count, suffix, width)
    return pl.pallas_call(
        unpack_kernel,
        out_shape=(
            jax.ShapeDtypeStruct(shape, arrived.dtype),
            jax.ShapeDtypeStruct((1, width), jnp.float32),
        ),
        in_specs=[pl.BlockSpec(memory_space=pltpu.SMEM), hbm, pl.BlockSpec(memory_space=pl.ANY)],
        out_specs=(hbm, pl.BlockSpec(memory_space=pltpu.VMEM)),
        scratch_shapes=[
            pltpu.VMEM(shape, arrived.dtype),
            pltpu.SemaphoreType.DMA((count,)),
            pltpu.SemaphoreType.DMA((CHUNKS,)),
        ],
        name="unpack",
    )(slots, arrived, other)


def finish_kernel(slots, arrived, counted, step, place, *refs):
    *parts, result, rung_means, next_lengths, held, in_sems, out_sems = refs

    def sums():
        shared = jnp.concatenate([part[...] for part in parts], axis=0)
        peaks, sums, filled = shared[:, 0], shared[:, 1], shared[:, 2]
        top = jnp.max(peaks, axis=0, keepdims=True)
        summed = jnp.sum(sums * jnp.exp(peaks - top), axis=0, keepdims=True)
        rung_means[...] = (top + jnp.log(summed) - jnp.log(counted[...]))[:, :RUNGS]
        order = lax.broadcasted_iota(jnp.int32, filled.shape, 0)
        owner = (order == step[...]).astype(jnp.float32)
        found = lax.dot_general(
            filled, owner, (((0,), (0,)), ((), ())), preferred_element_type=jnp.float32
        )
        order = lax.broadcasted_iota(jnp.int32, found.shape, 0)
        length = jnp.sum(jnp.where(order == place[...], found, 0.0), axis=0, keepdims=True)
        next_lengths[...] = length.astype(jnp.int32) + STEPS

    move_rows(slots, arrived, result, held, in_sems, out_sems, sums)


def finish(arrived, slots, parts, counted, step, place):
    count, (_, suffix, width) = slots.shape[0], arrived.shape
    hbm = pl.BlockSpec(memory_space=pltpu.HBM)
    vmem = pl.BlockSpec(memory_space=pltpu.VMEM)
    shape = (count, suffix, width)
    return pl.pallas_call(
        finish_kernel,
        out_shape=(
            jax.ShapeDtypeStruct(shape, arrived.dtype),
            jax.ShapeDtypeStruct((1, RUNGS), jnp.float32),
            jax.ShapeDtypeStruct(step.shape, jnp.int32),
        ),
        in_specs=[pl.BlockSpec(memory_space=pltpu.SMEM), hbm] + [vmem] * (3 + len(parts)),
        out_specs=(hbm, vmem, vmem),
        scratch_shapes=[
            pltpu.VMEM(shape, arrived.dtype),
            pltpu.SemaphoreType.DMA((count,)),
            pltpu.SemaphoreType.DMA((CHUNKS,)),
        ],
        name="finish",
    )(slots, arrived, counted, step, place, *parts)


def along(array, axes):
    sides = SIDES
    total = sides[0] * sides[1] * sides[2]
    parts = []
    for steps in itertools.product(*(range(sides[axis]) for axis in axes)):
        pairs = []
        for i in range(total):
            goal = [i // (sides[1] * sides[2]), i // sides[2] % sides[1], i % sides[2]]
            for axis, step in zip(axes, steps):
                goal[axis] = (goal[axis] + step) % sides[axis]
            pairs.append((i, (goal[0] * sides[1] + goal[1]) * sides[2] + goal[2]))
        parts.append(lax.ppermute(array, "particle", pairs) if any(steps) else array)
    return parts


def half_of(array):
    tall, wide, cores = SIDES
    parts = []
    for hop, step in itertools.product(range(2), range(2)):
        pairs = []
        for i in range(tall * wide * cores):
            y, x, core = i // (wide * cores), i // cores % wide, i % cores
            goal = (y ^ hop) * wide + (x + 2 * core + step) % wide
            pairs.append((i, goal * cores + core))
        parts.append(lax.ppermute(array, "particle", pairs))
    return parts


def shards(
    queries,
    new_keys,
    new_values,
    key_cache,
    value_cache,
    prompt_keys,
    prompt_values,
    lengths,
    prior,
    reward_dir,
    rungs,
    ancestors,
):
    per_device = queries.shape[0]
    suffix = key_cache.shape[1]
    groups = HEADS // KV_HEADS
    scale = HEAD_DIM ** (-0.5)
    sources = lax.axis_size("particle")
    device = lax.axis_index("particle")

    wanted = ancestors.reshape(sources, per_device)
    owner = wanted // per_device
    local = wanted % per_device
    chosen = owner == device
    least = jnp.min(jnp.where(chosen, local, per_device - 1), axis=1)
    most = jnp.max(jnp.where(chosen, local, 0), axis=1)
    mine = lax.dynamic_slice_in_dim(ancestors, device * per_device, per_device)
    mine_owner = mine // per_device
    same_owner = mine_owner[:, None] == mine_owner[None, :]
    first = jnp.min(jnp.where(same_owner, mine[None, :], sources * per_device), axis=1)
    slot = mine_owner * DISTINCT + (mine != first).astype(jnp.int32)

    low = -jnp.inf
    shard = jnp.maximum(
        jnp.pad(prompt_keys, ((0, 0), (0, HEAD_DIM)), constant_values=low),
        jnp.pad(prompt_values, ((0, 0), (HEAD_DIM, 0)), constant_values=low),
    )
    chip = jnp.concatenate(along(shard, (2,)), axis=0)
    chip = chip + jnp.minimum(least[0], 0).astype(chip.dtype)
    beside = lax.ppermute(chip, "particle", [(i, i ^ 16) for i in range(sources)])
    column = jnp.concatenate([chip, beside], axis=0)
    halves = half_of(column)

    exchange = functools.partial(
        lax.all_to_all, axis_name="particle", split_axis=0, concat_axis=0, tiled=True
    )
    places = (lengths, least, most)
    (outgoing_keys,) = pack((key_cache,), (new_keys,), *places, False)
    arrived_keys = exchange(after(outgoing_keys, column))
    outgoing_values, written_keys, written_values = pack(
        (key_cache, value_cache), (new_keys, new_values), *places, True
    )
    arrived_values = exchange(after(outgoing_values, arrived_keys))
    next_keys, mark = unpack(arrived_keys, slot, column)

    half = jnp.concatenate(halves, axis=0) + zero_after(arrived_keys)[0, 0].astype(shard.dtype)
    prompt = jnp.concatenate(along(half, (2,)), axis=0)
    all_keys = prompt[:, :HEAD_DIM]
    all_values = prompt[:, HEAD_DIM:]

    query = queries.reshape(per_device, STEPS, groups, HEAD_DIM)
    front = (
        jnp.einsum("pshd,nd->pshn", query, all_keys, preferred_element_type=jnp.float32) * scale
    )
    back = (
        jnp.einsum("pshd,pld->pshl", query, written_keys, preferred_element_type=jnp.float32)
        * scale
    )
    position = jnp.arange(suffix, dtype=jnp.int32)
    later = jnp.arange(STEPS, dtype=jnp.int32)
    visible = position[None, None, :] < lengths[:, None, None] + 1 + later[None, :, None]
    back = jnp.where(visible[:, :, None, :], back, -jnp.inf)
    peak = jnp.maximum(jnp.max(front, axis=-1), jnp.max(back, axis=-1))
    front = jnp.exp(front - peak[..., None])
    back = jnp.exp(back - peak[..., None])
    total = jnp.sum(front, axis=-1) + jnp.sum(back, axis=-1)
    mixed = jnp.einsum(
        "pshn,nd->pshd",
        front.astype(jnp.bfloat16),
        all_values,
        preferred_element_type=jnp.float32,
    ) + jnp.einsum(
        "pshl,pld->pshd",
        back.astype(jnp.bfloat16),
        written_values,
        preferred_element_type=jnp.float32,
    )
    output = (mixed / total[..., None]).reshape(per_device, STEPS, -1)
    attention = output.astype(jnp.bfloat16)

    partial_reward = jnp.sum(output * reward_dir[None, None, :], axis=(1, 2))
    reward = partial_reward
    for bit in (1, 2, 4):
        pairs = [(i, i ^ bit) for i in range(PLANES)]
        reward = reward + lax.ppermute(reward, "tensor", pairs)
    weights = prior + reward
    own_rungs = lax.dynamic_slice_in_dim(rungs, device * per_device, per_device)
    ladder = jnp.arange(RUNGS, dtype=jnp.int32)
    member = own_rungs[:, None] == ladder[None, :]
    local_peak = jnp.max(jnp.where(member, weights[:, None], -1e30), axis=0)
    local_sum = jnp.sum(
        jnp.where(member, jnp.exp(weights[:, None] - local_peak[None, :]), 0.0), axis=0
    )
    spare = per_device - RUNGS
    shared = jnp.stack(
        [
            jnp.pad(local_peak, (0, spare)),
            jnp.pad(local_sum, (0, spare), constant_values=1.0),
            lengths.astype(jnp.float32),
        ]
    )[None]
    near = jnp.concatenate(along(shared, (2,)), axis=0)
    near = after(near, attention, mark)
    near = jnp.concatenate(along(near, (0,)), axis=0)
    parts = along(near, (1,))

    counted = jnp.sum((rungs[:, None] == ladder[None, :]).astype(jnp.float32), axis=0)
    tall, wide, cores = SIDES
    up = (device // (wide * cores) - mine_owner // (wide * cores)) % tall
    right = (device // cores % wide - mine_owner // cores % wide) % wide
    across = (device % cores - mine_owner % cores) % cores
    step = (right * tall + up) * cores + across
    next_values, rung_means, next_lengths = finish(
        arrived_values,
        slot,
        parts,
        jnp.pad(counted, (0, spare), constant_values=1.0)[None],
        step[None],
        (mine % per_device)[None],
    )
    rung_means = rung_means[0]
    next_lengths = next_lengths[0]
    return (attention, weights, rung_means, next_keys, next_values, next_lengths)


def solution(mesh):
    placed = (
        P("particle", None, "tensor"),
        P("particle", None, "tensor"),
        P("particle", None, "tensor"),
        P("particle", None, "tensor"),
        P("particle", None, "tensor"),
        P("particle", "tensor"),
        P("particle", "tensor"),
        P("particle"),
        P("particle"),
        P("tensor"),
        P(),
        P(),
    )
    return jax.shard_map(
        shards,
        mesh=mesh,
        in_specs=placed,
        out_specs=(
            P("particle", None, "tensor"),
            P("particle"),
            P(),
            P("particle", None, "tensor"),
            P("particle", None, "tensor"),
            P("particle"),
        ),
        check_vma=False,
    )
```

```python
import functools
import itertools

import jax
import jax.numpy as jnp
from jax import lax
from jax.experimental import pallas as pl
from jax.experimental.pallas import tpu as pltpu
from jax.sharding import PartitionSpec as P

HEADS = 64
KV_HEADS = 8
HEAD_DIM = 128
STEPS = 2
RUNGS = 8
DISTINCT = 2
SIDES = (4, 4, 2)
PLANES = 8
WINDOW = 32
CHUNKS = 4
GROUP = 2


def pack_kernel(keeps, lengths, least, most, *refs):
    number = (len(refs) - 5) // (2 + keeps)
    caches, fresh, (packed, *written) = refs[:number], refs[number : 2 * number], refs[2 * number : -4]
    held, in_sems, out_sems, send_sems = refs[-4:]
    count, suffix, _ = caches[0].shape
    goals = least.shape[0]
    share = count // CHUNKS

    def load(chunk, n):
        rows = pl.ds(chunk * share, share)
        return pltpu.make_async_copy(
            caches[n].at[rows], held.at[n, rows], in_sems.at[chunk * number + n]
        )

    def keep(n):
        return pltpu.make_async_copy(held.at[n], written[n], out_sems.at[n])

    def low(d):
        return pltpu.make_async_copy(
            held.at[number - 1, least[d]], packed.at[2 * d], send_sems.at[2 * d]
        )

    def high(d):
        return pltpu.make_async_copy(
            held.at[number - 1, most[d]], packed.at[2 * d + 1], send_sems.at[2 * d + 1]
        )

    def each(d, act):
        pl.when(least[d] <= most[d])(lambda: act(low(d)))
        pl.when(least[d] < most[d])(lambda: act(high(d)))

    def patch(group):
        found = []
        for i in range(GROUP):
            p = group * GROUP + i
            length = lengths[p]
            base = pl.multiple_of(jnp.minimum(length // 16 * 16, suffix - WINDOW), 16)
            for n in range(number):
                place = (n, p, pl.ds(base, WINDOW))
                block = held[place].astype(jnp.float32)
                lines = fresh[n][p].astype(jnp.float32)
                row = lax.broadcasted_iota(jnp.int32, block.shape, 0) + base
                for offset in range(STEPS):
                    block = jnp.where(row == length + offset, lines[offset : offset + 1], block)
                found.append((place, block.astype(held.dtype)))
        for place, block in found:
            held[place] = block

    for chunk in range(CHUNKS):
        for n in range(number):
            load(chunk, n).start()
    for chunk in range(CHUNKS):
        for n in range(number):
            load(chunk, n).wait()
        groups = share // GROUP
        repeat(groups, lambda g, chunk=chunk: patch(g + chunk * groups), 1)
    repeat(goals, lambda d: each(d, lambda copy: copy.start()))
    for n in range(number * keeps):
        keep(n).start()
    repeat(goals, lambda d: each(d, lambda copy: copy.wait()))
    for n in range(number * keeps):
        keep(n).wait()


def repeat(count, body, unroll=4):
    def step(i, carry):
        body(i)
        return carry

    lax.fori_loop(0, count, step, 0, unroll=unroll)


def pack(caches, fresh, lengths, least, most, keeps):
    cache, number = caches[0], len(caches)
    count, goals = cache.shape[0], least.shape[0]
    smem = pl.BlockSpec(memory_space=pltpu.SMEM)
    hbm = pl.BlockSpec(memory_space=pltpu.HBM)
    vmem = pl.BlockSpec(memory_space=pltpu.VMEM)
    return pl.pallas_call(
        functools.partial(pack_kernel, keeps),
        out_shape=[jax.ShapeDtypeStruct((goals * DISTINCT,) + cache.shape[1:], cache.dtype)]
        + [jax.ShapeDtypeStruct(cache.shape, cache.dtype)] * (number * keeps),
        in_specs=[smem] * 3 + [hbm] * number + [vmem] * number,
        out_specs=[hbm] * (1 + number * keeps),
        scratch_shapes=[
            pltpu.VMEM((number,) + cache.shape, cache.dtype),
            pltpu.SemaphoreType.DMA((number * CHUNKS,)),
            pltpu.SemaphoreType.DMA((number,)),
            pltpu.SemaphoreType.DMA((goals * DISTINCT,)),
        ],
        name="pack",
    )(lengths, least, most, *caches, *fresh)


def after(array, *others):
    hbm = pl.BlockSpec(memory_space=pltpu.HBM)
    return pl.pallas_call(
        lambda *refs: None,
        out_shape=jax.ShapeDtypeStruct(array.shape, array.dtype),
        in_specs=[hbm] + [pl.BlockSpec(memory_space=pl.ANY)] * len(others),
        out_specs=hbm,
        input_output_aliases={0: 0},
        name="after",
    )(array, *others)


def zero_kernel(_, zero):
    zero[...] = jnp.zeros_like(zero)


def zero_after(array):
    return pl.pallas_call(
        zero_kernel,
        out_shape=jax.ShapeDtypeStruct((1, HEAD_DIM), jnp.float32),
        in_specs=[pl.BlockSpec(memory_space=pltpu.HBM)],
        out_specs=pl.BlockSpec(memory_space=pltpu.VMEM),
        name="zero",
    )(array)


def move_rows(slots, arrived, result, held, in_sems, out_sems, meanwhile):
    count = result.shape[0]
    share = count // CHUNKS

    def load(p):
        return pltpu.make_async_copy(arrived.at[slots[p]], held.at[p], in_sems.at[p])

    def keep(chunk):
        rows = pl.ds(chunk * share, share)
        return pltpu.make_async_copy(held.at[rows], result.at[rows], out_sems.at[chunk])

    repeat(count, lambda p: load(p).start(), count)
    meanwhile()
    for chunk in range(CHUNKS):
        repeat(share, lambda p, chunk=chunk: load(p + chunk * share).wait(), share)
        keep(chunk).start()
    for chunk in range(CHUNKS):
        keep(chunk).wait()


def unpack_kernel(slots, arrived, _, result, mark, held, in_sems, out_sems):
    def clear():
        mark[...] = jnp.zeros_like(mark)

    move_rows(slots, arrived, result, held, in_sems, out_sems, clear)


def unpack(arrived, slots, other):
    count, (_, suffix, width) = slots.shape[0], arrived.shape
    hbm = pl.BlockSpec(memory_space=pltpu.HBM)
    shape = (count, suffix, width)
    return pl.pallas_call(
        unpack_kernel,
        out_shape=(
            jax.ShapeDtypeStruct(shape, arrived.dtype),
            jax.ShapeDtypeStruct((1, width), jnp.float32),
        ),
        in_specs=[pl.BlockSpec(memory_space=pltpu.SMEM), hbm, pl.BlockSpec(memory_space=pl.ANY)],
        out_specs=(hbm, pl.BlockSpec(memory_space=pltpu.VMEM)),
        scratch_shapes=[
            pltpu.VMEM(shape, arrived.dtype),
            pltpu.SemaphoreType.DMA((count,)),
            pltpu.SemaphoreType.DMA((CHUNKS,)),
        ],
        name="unpack",
    )(slots, arrived, other)


def finish_kernel(slots, arrived, counted, step, place, *refs):
    *parts, result, rung_means, next_lengths, held, in_sems, out_sems = refs

    def sums():
        shared = jnp.concatenate([part[...] for part in parts], axis=0)
        peaks, sums, filled = shared[:, 0], shared[:, 1], shared[:, 2]
        top = jnp.max(peaks, axis=0, keepdims=True)
        summed = jnp.sum(sums * jnp.exp(peaks - top), axis=0, keepdims=True)
        rung_means[...] = (top + jnp.log(summed) - jnp.log(counted[...]))[:, :RUNGS]
        order = lax.broadcasted_iota(jnp.int32, filled.shape, 0)
        owner = (order == step[...]).astype(jnp.float32)
        found = lax.dot_general(
            filled, owner, (((0,), (0,)), ((), ())), preferred_element_type=jnp.float32
        )
        order = lax.broadcasted_iota(jnp.int32, found.shape, 0)
        length = jnp.sum(jnp.where(order == place[...], found, 0.0), axis=0, keepdims=True)
        next_lengths[...] = length.astype(jnp.int32) + STEPS

    move_rows(slots, arrived, result, held, in_sems, out_sems, sums)


def finish(arrived, slots, parts, counted, step, place):
    count, (_, suffix, width) = slots.shape[0], arrived.shape
    hbm = pl.BlockSpec(memory_space=pltpu.HBM)
    vmem = pl.BlockSpec(memory_space=pltpu.VMEM)
    shape = (count, suffix, width)
    return pl.pallas_call(
        finish_kernel,
        out_shape=(
            jax.ShapeDtypeStruct(shape, arrived.dtype),
            jax.ShapeDtypeStruct((1, RUNGS), jnp.float32),
            jax.ShapeDtypeStruct(step.shape, jnp.int32),
        ),
        in_specs=[pl.BlockSpec(memory_space=pltpu.SMEM), hbm] + [vmem] * (3 + len(parts)),
        out_specs=(hbm, vmem, vmem),
        scratch_shapes=[
            pltpu.VMEM(shape, arrived.dtype),
            pltpu.SemaphoreType.DMA((count,)),
            pltpu.SemaphoreType.DMA((CHUNKS,)),
        ],
        name="finish",
    )(slots, arrived, counted, step, place, *parts)


def along(array, axes):
    sides = SIDES
    total = sides[0] * sides[1] * sides[2]
    parts = []
    for steps in itertools.product(*(range(sides[axis]) for axis in axes)):
        pairs = []
        for i in range(total):
            goal = [i // (sides[1] * sides[2]), i // sides[2] % sides[1], i % sides[2]]
            for axis, step in zip(axes, steps):
                goal[axis] ^= step
            pairs.append((i, (goal[0] * sides[1] + goal[1]) * sides[2] + goal[2]))
        parts.append(lax.ppermute(array, "particle", pairs) if any(steps) else array)
    return parts


def half_of(array):
    tall, wide, cores = SIDES
    parts = []
    for hop, step in itertools.product(range(2), range(2)):
        pairs = []
        for i in range(tall * wide * cores):
            y, x, core = i // (wide * cores), i // cores % wide, i % cores
            goal = (y ^ hop) * wide + (x ^ (2 * core + step))
            pairs.append((i, goal * cores + core))
        parts.append(lax.ppermute(array, "particle", pairs))
    return parts


def shards(
    queries,
    new_keys,
    new_values,
    key_cache,
    value_cache,
    prompt_keys,
    prompt_values,
    lengths,
    prior,
    reward_dir,
    rungs,
    ancestors,
):
    per_device = queries.shape[0]
    suffix = key_cache.shape[1]
    groups = HEADS // KV_HEADS
    scale = HEAD_DIM ** (-0.5)
    sources = lax.axis_size("particle")
    device = lax.axis_index("particle")

    wanted = ancestors.reshape(sources, per_device)
    owner = wanted // per_device
    local = wanted % per_device
    chosen = owner == device
    least = jnp.min(jnp.where(chosen, local, per_device - 1), axis=1)
    most = jnp.max(jnp.where(chosen, local, 0), axis=1)
    mine = lax.dynamic_slice_in_dim(ancestors, device * per_device, per_device)
    mine_owner = mine // per_device
    same_owner = mine_owner[:, None] == mine_owner[None, :]
    first = jnp.min(jnp.where(same_owner, mine[None, :], sources * per_device), axis=1)
    slot = mine_owner * DISTINCT + (mine != first).astype(jnp.int32)

    low = -jnp.inf
    shard = jnp.maximum(
        jnp.pad(prompt_keys, ((0, 0), (0, HEAD_DIM)), constant_values=low),
        jnp.pad(prompt_values, ((0, 0), (HEAD_DIM, 0)), constant_values=low),
    )
    chip = jnp.concatenate(along(shard, (2,)), axis=0)
    chip = chip + jnp.minimum(least[0], 0).astype(chip.dtype)
    beside = lax.ppermute(chip, "particle", [(i, i ^ 16) for i in range(sources)])
    column = jnp.concatenate([chip, beside], axis=0)
    halves = half_of(column)

    exchange = functools.partial(
        lax.all_to_all, axis_name="particle", split_axis=0, concat_axis=0, tiled=True
    )
    places = (lengths, least, most)
    (outgoing_keys,) = pack((key_cache,), (new_keys,), *places, False)
    arrived_keys = exchange(after(outgoing_keys, beside))
    outgoing_values, written_keys, written_values = pack(
        (key_cache, value_cache), (new_keys, new_values), *places, True
    )
    arrived_values = exchange(after(outgoing_values, arrived_keys))
    next_keys, mark = unpack(arrived_keys, slot, column)

    half = jnp.concatenate(halves, axis=0) + zero_after(arrived_keys)[0, 0].astype(shard.dtype)
    prompt = jnp.concatenate(along(half, (2,)), axis=0)
    all_keys = prompt[:, :HEAD_DIM]
    all_values = prompt[:, HEAD_DIM:]

    query = queries.reshape(per_device, STEPS, groups, HEAD_DIM)
    front = (
        jnp.einsum("pshd,nd->pshn", query, all_keys, preferred_element_type=jnp.float32) * scale
    )
    back = (
        jnp.einsum("pshd,pld->pshl", query, written_keys, preferred_element_type=jnp.float32)
        * scale
    )
    position = jnp.arange(suffix, dtype=jnp.int32)
    later = jnp.arange(STEPS, dtype=jnp.int32)
    visible = position[None, None, :] < lengths[:, None, None] + 1 + later[None, :, None]
    back = jnp.where(visible[:, :, None, :], back, -jnp.inf)
    peak = jnp.maximum(jnp.max(front, axis=-1), jnp.max(back, axis=-1))
    front = jnp.exp(front - peak[..., None])
    back = jnp.exp(back - peak[..., None])
    total = jnp.sum(front, axis=-1) + jnp.sum(back, axis=-1)
    mixed = jnp.einsum(
        "pshn,nd->pshd",
        front.astype(jnp.bfloat16),
        all_values,
        preferred_element_type=jnp.float32,
    ) + jnp.einsum(
        "pshl,pld->pshd",
        back.astype(jnp.bfloat16),
        written_values,
        preferred_element_type=jnp.float32,
    )
    output = (mixed / total[..., None]).reshape(per_device, STEPS, -1)
    attention = output.astype(jnp.bfloat16)

    partial_reward = jnp.sum(output * reward_dir[None, None, :], axis=(1, 2))
    reward = partial_reward
    for bit in (1, 2, 4):
        pairs = [(i, i ^ bit) for i in range(PLANES)]
        reward = reward + lax.ppermute(reward, "tensor", pairs)
    weights = prior + reward
    own_rungs = lax.dynamic_slice_in_dim(rungs, device * per_device, per_device)
    ladder = jnp.arange(RUNGS, dtype=jnp.int32)
    member = own_rungs[:, None] == ladder[None, :]
    local_peak = jnp.max(jnp.where(member, weights[:, None], -1e30), axis=0)
    local_sum = jnp.sum(
        jnp.where(member, jnp.exp(weights[:, None] - local_peak[None, :]), 0.0), axis=0
    )
    spare = per_device - RUNGS
    shared = jnp.stack(
        [
            jnp.pad(local_peak, (0, spare)),
            jnp.pad(local_sum, (0, spare), constant_values=1.0),
            lengths.astype(jnp.float32),
        ]
    )[None]
    near = jnp.concatenate(along(shared, (2,)), axis=0)
    near = after(near, attention, mark)
    near = jnp.concatenate(along(near, (0,)), axis=0)
    parts = along(near, (1,))

    counted = jnp.sum((rungs[:, None] == ladder[None, :]).astype(jnp.float32), axis=0)
    tall, wide, cores = SIDES
    up = (device // (wide * cores)) ^ (mine_owner // (wide * cores))
    right = (device // cores % wide) ^ (mine_owner // cores % wide)
    across = (device % cores) ^ (mine_owner % cores)
    step = (right * tall + up) * cores + across
    next_values, rung_means, next_lengths = finish(
        arrived_values,
        slot,
        parts,
        jnp.pad(counted, (0, spare), constant_values=1.0)[None],
        step[None],
        (mine % per_device)[None],
    )
    rung_means = rung_means[0]
    next_lengths = next_lengths[0]
    return (attention, weights, rung_means, next_keys, next_values, next_lengths)


def solution(mesh):
    placed = (
        P("particle", None, "tensor"),
        P("particle", None, "tensor"),
        P("particle", None, "tensor"),
        P("particle", None, "tensor"),
        P("particle", None, "tensor"),
        P("particle", "tensor"),
        P("particle", "tensor"),
        P("particle"),
        P("particle"),
        P("tensor"),
        P(),
        P(),
    )
    return jax.shard_map(
        shards,
        mesh=mesh,
        in_specs=placed,
        out_specs=(
            P("particle", None, "tensor"),
            P("particle"),
            P(),
            P("particle", None, "tensor"),
            P("particle", None, "tensor"),
            P("particle"),
        ),
        check_vma=False,
    )
```

```python
import functools
import itertools

import jax
import jax.numpy as jnp
from jax import lax
from jax.experimental import pallas as pl
from jax.experimental.pallas import tpu as pltpu
from jax.sharding import PartitionSpec as P

HEADS = 64
KV_HEADS = 8
HEAD_DIM = 128
STEPS = 2
RUNGS = 8
DISTINCT = 2
SIDES = (4, 4, 2)
PLANES = 8
WINDOW = 32
CHUNKS = 4
SHARE = 8
GROUP = 2


def pack_kernel(keeps, lengths, least, most, *refs):
    number = (len(refs) - 5) // (2 + keeps)
    caches, fresh, (packed, *written) = refs[:number], refs[number : 2 * number], refs[2 * number : -4]
    held, in_sems, out_sems, send_sems = refs[-4:]
    count, suffix, _ = caches[0].shape
    goals = least.shape[0]
    share = count // CHUNKS

    def load(chunk, n):
        rows = pl.ds(chunk * share, share)
        return pltpu.make_async_copy(
            caches[n].at[rows], held.at[n, rows], in_sems.at[chunk * number + n]
        )

    def keep(n):
        return pltpu.make_async_copy(held.at[n], written[n], out_sems.at[n])

    def low(d):
        return pltpu.make_async_copy(
            held.at[number - 1, least[d]], packed.at[2 * d], send_sems.at[2 * d]
        )

    def high(d):
        return pltpu.make_async_copy(
            held.at[number - 1, most[d]], packed.at[2 * d + 1], send_sems.at[2 * d + 1]
        )

    def each(d, act):
        pl.when(least[d] <= most[d])(lambda: act(low(d)))
        pl.when(least[d] < most[d])(lambda: act(high(d)))

    def patch(group):
        found = []
        for i in range(GROUP):
            p = group * GROUP + i
            length = lengths[p]
            base = pl.multiple_of(jnp.minimum(length // 16 * 16, suffix - WINDOW), 16)
            for n in range(number):
                place = (n, p, pl.ds(base, WINDOW))
                block = held[place].astype(jnp.float32)
                lines = fresh[n][p].astype(jnp.float32)
                row = lax.broadcasted_iota(jnp.int32, block.shape, 0) + base
                for offset in range(STEPS):
                    block = jnp.where(row == length + offset, lines[offset : offset + 1], block)
                found.append((place, block.astype(held.dtype)))
        for place, block in found:
            held[place] = block

    for chunk in range(CHUNKS):
        for n in range(number):
            load(chunk, n).start()
    for chunk in range(CHUNKS):
        for n in range(number):
            load(chunk, n).wait()
        groups = share // GROUP
        repeat(groups, lambda g, chunk=chunk: patch(g + chunk * groups), 1)
    repeat(goals, lambda d: each(d, lambda copy: copy.start()))
    for n in range(number * keeps):
        keep(n).start()
    repeat(goals, lambda d: each(d, lambda copy: copy.wait()))
    for n in range(number * keeps):
        keep(n).wait()


def repeat(count, body, unroll=4):
    def step(i, carry):
        body(i)
        return carry

    lax.fori_loop(0, count, step, 0, unroll=unroll)


def pack(caches, fresh, lengths, least, most, keeps):
    cache, number = caches[0], len(caches)
    count, goals = cache.shape[0], least.shape[0]
    smem = pl.BlockSpec(memory_space=pltpu.SMEM)
    hbm = pl.BlockSpec(memory_space=pltpu.HBM)
    vmem = pl.BlockSpec(memory_space=pltpu.VMEM)
    return pl.pallas_call(
        functools.partial(pack_kernel, keeps),
        out_shape=[jax.ShapeDtypeStruct((goals * DISTINCT,) + cache.shape[1:], cache.dtype)]
        + [jax.ShapeDtypeStruct(cache.shape, cache.dtype)] * (number * keeps),
        in_specs=[smem] * 3 + [hbm] * number + [vmem] * number,
        out_specs=[hbm] * (1 + number * keeps),
        scratch_shapes=[
            pltpu.VMEM((number,) + cache.shape, cache.dtype),
            pltpu.SemaphoreType.DMA((number * CHUNKS,)),
            pltpu.SemaphoreType.DMA((number,)),
            pltpu.SemaphoreType.DMA((goals * DISTINCT,)),
        ],
        name="pack",
    )(lengths, least, most, *caches, *fresh)


def after(array, *others):
    hbm = pl.BlockSpec(memory_space=pltpu.HBM)
    return pl.pallas_call(
        lambda *refs: None,
        out_shape=jax.ShapeDtypeStruct(array.shape, array.dtype),
        in_specs=[hbm] + [pl.BlockSpec(memory_space=pl.ANY)] * len(others),
        out_specs=hbm,
        input_output_aliases={0: 0},
        name="after",
    )(array, *others)


def zero_kernel(_, zero):
    zero[...] = jnp.zeros_like(zero)


def zero_after(array):
    return pl.pallas_call(
        zero_kernel,
        out_shape=jax.ShapeDtypeStruct((1, HEAD_DIM), jnp.float32),
        in_specs=[pl.BlockSpec(memory_space=pltpu.HBM)],
        out_specs=pl.BlockSpec(memory_space=pltpu.VMEM),
        name="zero",
    )(array)


def move_rows(slots, arrived, result, held, in_sems, out_sems, meanwhile, first, last):
    share = SHARE

    def load(p):
        return pltpu.make_async_copy(arrived.at[slots[p]], held.at[p], in_sems.at[p])

    def keep(chunk):
        rows = pl.ds(chunk * share, share)
        return pltpu.make_async_copy(held.at[rows], result.at[rows], out_sems.at[chunk])

    chunks = range(first // share, last // share)
    repeat(last - first, lambda p: load(p + first).start(), last - first)
    meanwhile()
    for chunk in chunks:
        repeat(share, lambda p, chunk=chunk: load(p + chunk * share).wait(), share)
        keep(chunk).start()
    for chunk in chunks:
        keep(chunk).wait()


def unpack_kernel(last, slots, arrived, _, result, mark, held, in_sems, out_sems):
    def clear():
        mark[...] = jnp.zeros_like(mark)

    move_rows(slots, arrived, result, held, in_sems, out_sems, clear, 0, last)


def unpack(arrived, slots, other, last):
    count, (_, suffix, width) = slots.shape[0], arrived.shape
    hbm = pl.BlockSpec(memory_space=pltpu.HBM)
    shape = (count, suffix, width)
    return pl.pallas_call(
        functools.partial(unpack_kernel, last),
        out_shape=(
            jax.ShapeDtypeStruct(shape, arrived.dtype),
            jax.ShapeDtypeStruct((1, width), jnp.float32),
        ),
        in_specs=[pl.BlockSpec(memory_space=pltpu.SMEM), hbm, pl.BlockSpec(memory_space=pl.ANY)],
        out_specs=(hbm, pl.BlockSpec(memory_space=pltpu.VMEM)),
        scratch_shapes=[
            pltpu.VMEM(shape, arrived.dtype),
            pltpu.SemaphoreType.DMA((count,)),
            pltpu.SemaphoreType.DMA((CHUNKS,)),
        ],
        name="unpack",
    )(slots, arrived, other)


def finish_kernel(first, slots, arrived, _, counted, step, place, *refs):
    *parts, result, rung_means, next_lengths, held, in_sems, out_sems = refs

    def sums():
        shared = jnp.concatenate([part[...] for part in parts], axis=0)
        peaks, sums, filled = shared[:, 0], shared[:, 1], shared[:, 2]
        top = jnp.max(peaks, axis=0, keepdims=True)
        summed = jnp.sum(sums * jnp.exp(peaks - top), axis=0, keepdims=True)
        rung_means[...] = (top + jnp.log(summed) - jnp.log(counted[...]))[:, :RUNGS]
        order = lax.broadcasted_iota(jnp.int32, filled.shape, 0)
        owner = (order == step[...]).astype(jnp.float32)
        found = lax.dot_general(
            filled, owner, (((0,), (0,)), ((), ())), preferred_element_type=jnp.float32
        )
        order = lax.broadcasted_iota(jnp.int32, found.shape, 0)
        length = jnp.sum(jnp.where(order == place[...], found, 0.0), axis=0, keepdims=True)
        next_lengths[...] = length.astype(jnp.int32) + STEPS

    last = result.shape[0]
    move_rows(slots, arrived, result, held, in_sems, out_sems, sums, first, last)


def finish(arrived, slots, begun, first, parts, counted, step, place):
    count, (_, suffix, width) = slots.shape[0], arrived.shape
    hbm = pl.BlockSpec(memory_space=pltpu.HBM)
    vmem = pl.BlockSpec(memory_space=pltpu.VMEM)
    shape = (count, suffix, width)
    return pl.pallas_call(
        functools.partial(finish_kernel, first),
        out_shape=(
            jax.ShapeDtypeStruct(shape, arrived.dtype),
            jax.ShapeDtypeStruct((1, RUNGS), jnp.float32),
            jax.ShapeDtypeStruct(step.shape, jnp.int32),
        ),
        in_specs=[pl.BlockSpec(memory_space=pltpu.SMEM), hbm, hbm] + [vmem] * (3 + len(parts)),
        out_specs=(hbm, vmem, vmem),
        scratch_shapes=[
            pltpu.VMEM(shape, arrived.dtype),
            pltpu.SemaphoreType.DMA((count,)),
            pltpu.SemaphoreType.DMA((CHUNKS,)),
        ],
        input_output_aliases={2: 0},
        name="finish",
    )(slots, arrived, begun, counted, step, place, *parts)


def along(array, axes):
    sides = SIDES
    total = sides[0] * sides[1] * sides[2]
    parts = []
    for steps in itertools.product(*(range(sides[axis]) for axis in axes)):
        pairs = []
        for i in range(total):
            goal = [i // (sides[1] * sides[2]), i // sides[2] % sides[1], i % sides[2]]
            for axis, step in zip(axes, steps):
                goal[axis] = (goal[axis] + step) % sides[axis]
            pairs.append((i, (goal[0] * sides[1] + goal[1]) * sides[2] + goal[2]))
        parts.append(lax.ppermute(array, "particle", pairs) if any(steps) else array)
    return parts


def half_of(array):
    tall, wide, cores = SIDES
    parts = []
    for hop, step in itertools.product(range(2), range(2)):
        pairs = []
        for i in range(tall * wide * cores):
            y, x, core = i // (wide * cores), i // cores % wide, i % cores
            goal = (y ^ hop) * wide + (x + 2 * core + step) % wide
            pairs.append((i, goal * cores + core))
        parts.append(lax.ppermute(array, "particle", pairs))
    return parts


def shards(
    queries,
    new_keys,
    new_values,
    key_cache,
    value_cache,
    prompt_keys,
    prompt_values,
    lengths,
    prior,
    reward_dir,
    rungs,
    ancestors,
):
    per_device = queries.shape[0]
    suffix = key_cache.shape[1]
    groups = HEADS // KV_HEADS
    scale = HEAD_DIM ** (-0.5)
    sources = lax.axis_size("particle")
    device = lax.axis_index("particle")

    wanted = ancestors.reshape(sources, per_device)
    owner = wanted // per_device
    local = wanted % per_device
    chosen = owner == device
    least = jnp.min(jnp.where(chosen, local, per_device - 1), axis=1)
    most = jnp.max(jnp.where(chosen, local, 0), axis=1)
    mine = lax.dynamic_slice_in_dim(ancestors, device * per_device, per_device)
    mine_owner = mine // per_device
    same_owner = mine_owner[:, None] == mine_owner[None, :]
    first = jnp.min(jnp.where(same_owner, mine[None, :], sources * per_device), axis=1)
    slot = mine_owner * DISTINCT + (mine != first).astype(jnp.int32)

    low = -jnp.inf
    shard = jnp.maximum(
        jnp.pad(prompt_keys, ((0, 0), (0, HEAD_DIM)), constant_values=low),
        jnp.pad(prompt_values, ((0, 0), (HEAD_DIM, 0)), constant_values=low),
    )
    chip = jnp.concatenate(along(shard, (2,)), axis=0)
    chip = chip + jnp.minimum(least[0], 0).astype(chip.dtype)
    beside = lax.ppermute(chip, "particle", [(i, i ^ 16) for i in range(sources)])
    column = jnp.concatenate([chip, beside], axis=0)
    halves = half_of(column)

    exchange = functools.partial(
        lax.all_to_all, axis_name="particle", split_axis=0, concat_axis=0, tiled=True
    )
    places = (lengths, least, most)
    (outgoing_keys,) = pack((key_cache,), (new_keys,), *places, False)
    arrived_keys = exchange(after(outgoing_keys, column))
    outgoing_values, written_keys, written_values = pack(
        (key_cache, value_cache), (new_keys, new_values), *places, True
    )
    arrived_values = exchange(after(outgoing_values, arrived_keys))
    next_keys, mark = unpack(arrived_keys, slot, column, per_device)

    half = jnp.concatenate(halves, axis=0) + zero_after(arrived_keys)[0, 0].astype(shard.dtype)
    prompt = jnp.concatenate(along(half, (2,)), axis=0)
    all_keys = prompt[:, :HEAD_DIM]
    all_values = prompt[:, HEAD_DIM:]

    query = queries.reshape(per_device, STEPS, groups, HEAD_DIM)
    front = (
        jnp.einsum("pshd,nd->pshn", query, all_keys, preferred_element_type=jnp.float32) * scale
    )
    back = (
        jnp.einsum("pshd,pld->pshl", query, written_keys, preferred_element_type=jnp.float32)
        * scale
    )
    position = jnp.arange(suffix, dtype=jnp.int32)
    later = jnp.arange(STEPS, dtype=jnp.int32)
    visible = position[None, None, :] < lengths[:, None, None] + 1 + later[None, :, None]
    back = jnp.where(visible[:, :, None, :], back, -jnp.inf)
    peak = jnp.maximum(jnp.max(front, axis=-1), jnp.max(back, axis=-1))
    front = jnp.exp(front - peak[..., None])
    back = jnp.exp(back - peak[..., None])
    total = jnp.sum(front, axis=-1) + jnp.sum(back, axis=-1)
    mixed = jnp.einsum(
        "pshn,nd->pshd",
        front.astype(jnp.bfloat16),
        all_values,
        preferred_element_type=jnp.float32,
    ) + jnp.einsum(
        "pshl,pld->pshd",
        back.astype(jnp.bfloat16),
        written_values,
        preferred_element_type=jnp.float32,
    )
    output = (mixed / total[..., None]).reshape(per_device, STEPS, -1)
    attention = output.astype(jnp.bfloat16)

    partial_reward = jnp.sum(output * reward_dir[None, None, :], axis=(1, 2))
    reward = partial_reward
    for bit in (1, 2, 4):
        pairs = [(i, i ^ bit) for i in range(PLANES)]
        reward = reward + lax.ppermute(reward, "tensor", pairs)
    weights = prior + reward
    own_rungs = lax.dynamic_slice_in_dim(rungs, device * per_device, per_device)
    ladder = jnp.arange(RUNGS, dtype=jnp.int32)
    member = own_rungs[:, None] == ladder[None, :]
    local_peak = jnp.max(jnp.where(member, weights[:, None], -1e30), axis=0)
    local_sum = jnp.sum(
        jnp.where(member, jnp.exp(weights[:, None] - local_peak[None, :]), 0.0), axis=0
    )
    spare = per_device - RUNGS
    shared = jnp.stack(
        [
            jnp.pad(local_peak, (0, spare)),
            jnp.pad(local_sum, (0, spare), constant_values=1.0),
            lengths.astype(jnp.float32),
        ]
    )[None]
    near = jnp.concatenate(along(shared, (2,)), axis=0)
    near = after(near, attention, mark)
    near = jnp.concatenate(along(near, (0,)), axis=0)
    parts = along(near, (1,))

    counted = jnp.sum((rungs[:, None] == ladder[None, :]).astype(jnp.float32), axis=0)
    tall, wide, cores = SIDES
    up = (device // (wide * cores) - mine_owner // (wide * cores)) % tall
    right = (device // cores % wide - mine_owner // cores % wide) % wide
    across = (device % cores - mine_owner % cores) % cores
    step = (right * tall + up) * cores + across
    begun, _ = unpack(arrived_values, slot, near, per_device // 2)
    next_values, rung_means, next_lengths = finish(
        arrived_values,
        slot,
        begun,
        per_device // 2,
        parts,
        jnp.pad(counted, (0, spare), constant_values=1.0)[None],
        step[None],
        (mine % per_device)[None],
    )
    rung_means = rung_means[0]
    next_lengths = next_lengths[0]
    return (attention, weights, rung_means, next_keys, next_values, next_lengths)


def solution(mesh):
    placed = (
        P("particle", None, "tensor"),
        P("particle", None, "tensor"),
        P("particle", None, "tensor"),
        P("particle", None, "tensor"),
        P("particle", None, "tensor"),
        P("particle", "tensor"),
        P("particle", "tensor"),
        P("particle"),
        P("particle"),
        P("tensor"),
        P(),
        P(),
    )
    return jax.shard_map(
        shards,
        mesh=mesh,
        in_specs=placed,
        out_specs=(
            P("particle", None, "tensor"),
            P("particle"),
            P(),
            P("particle", None, "tensor"),
            P("particle", None, "tensor"),
            P("particle"),
        ),
        check_vma=False,
    )
```
